128 devices in a mesh: depth: 32 (over z, y_lo, x), head: 4 (over y_hi, core).
Axes of the slice: x: 4, y: 4 (y_hi: 2, y_lo: 2; y = y_hi * 2 + y_lo), z: 4, core: 2. Of those that a mesh axis runs over, the one named last changes fastest.
Arguments:
- embedded_homologs: bfloat16 [1024, 256, 768], P('depth'), may hold values from -6 to 6
- group_active_tallies: int32 [128], P('depth'), may hold values from 1 to 8
- asking_projector: bfloat16 [768, 768], P(None, 'head'), may hold values from -0.21875 to 0.21875
- lookup_projector: bfloat16 [768, 768], P(None, 'head'), may hold values from -0.21875 to 0.21875
- content_projector: bfloat16 [768, 768], P(None, 'head'), may hold values from -0.21875 to 0.21875
- contact_inner_matrix: float32 [12, 288], replicated, may hold values from -1.75 to 1.75
- contact_inner_offset: float32 [288], replicated, may hold values from -3 to 3
- contact_outer_matrix: float32 [288, 288], replicated, may hold values from -0.375 to 0.375
Outputs:
- attended: bfloat16 [1024, 256, 768], P('depth', None, 'head')
- pair: bfloat16 [256, 256, 288], P('head', 'depth')
The draws below stay inside these ranges and needn't reach their ends.
All inputs are finite; a program needn't handle non-finite values.
Results may differ from the reference program's by a relative error of at most 0.0071.
Values may be sent and summed in bfloat16 or wider, within the bound.
A program may use at most 64 MiB of HBM per device.

```python
import jax
import jax.numpy as jnp
from jax import lax

EMBED_SIZE = 768
HEADS = 12
HEAD_DIM = 64
SITE_TOTAL = 256
PAIR = 288
BLOCK = 8
SEQUENCES_EACH = 32
SEQUENCE_TOTAL = 1024
ROW_BLOCKS = 128


def draw_embedded_homologs(key, part):
    key = jax.random.fold_in(key, 11)
    first = jax.random.fold_in(key, 0)
    base = jax.random.normal(first, (SEQUENCE_TOTAL, SITE_TOTAL, EMBED_SIZE), jnp.float32)
    return jnp.clip(base, -6.0, 6.0).astype(jnp.bfloat16)


def with_ends(array, key, least, top_value):
    dims = array.shape
    place = [jax.random.randint(jax.random.fold_in(key, axis), (), 0, dims[axis]) for axis in range(len(dims))]
    array = array.at[tuple(place)].set(least)
    longest = dims.index(max(dims))
    place[longest] = (place[longest] + 1) % dims[longest]
    return array.at[tuple(place)].set(top_value)


def steps_of(rng, dims, cuts, least, top_value):
    factor_of, own = 1.0, jax.random.fold_in(rng, 6)
    for dim, shards_of in cuts:
        draws = jnp.exp(jax.random.uniform(jax.random.fold_in(own, dim), (shards_of,), jnp.float32, least / len(cuts), top_value / len(cuts)))
        factor_of = factor_of * jnp.repeat(draws, dims[dim] // shards_of).reshape([-1 if axis == dim else 1 for axis in range(len(dims))])
    return factor_of


def normal_values(key, shape, width, limit, shards=(), kind=jnp.bfloat16):
    level = steps_of(key, shape, shards, -0.22, 0.18) if shards else 1.0
    values = jax.random.normal(key, shape, jnp.float32) * width * level
    return jnp.minimum(jnp.maximum(values, -limit), limit).astype(kind)


def setup_inputs(seed: int = 0) -> dict:
    seeds = jax.random.split(jax.random.key(seed), 9)
    embedded_homologs = draw_embedded_homologs(jax.random.fold_in(seeds[8], 71), 0)
    group_active_tallies = with_ends(jax.random.randint(seeds[1], (ROW_BLOCKS,), 1, BLOCK + 1), jax.random.fold_in(seeds[1], 1), 1, BLOCK).astype(jnp.int32)
    asking_projector = normal_values(seeds[2], (EMBED_SIZE, EMBED_SIZE), EMBED_SIZE ** -0.5, 0.21875, ((1, 4),))
    lookup_projector = normal_values(seeds[3], (EMBED_SIZE, EMBED_SIZE), EMBED_SIZE ** -0.5, 0.21875, ((1, 4),))
    content_projector = normal_values(seeds[4], (EMBED_SIZE, EMBED_SIZE), EMBED_SIZE ** -0.5, 0.21875, ((1, 4),))
    contact_inner_matrix = normal_values(seeds[5], (HEADS, PAIR), HEADS ** -0.5, 1.75, (), jnp.float32)
    contact_inner_offset = normal_values(seeds[6], (PAIR,), 0.5, 3.0, (), jnp.float32)
    contact_outer_matrix = normal_values(seeds[7], (PAIR, PAIR), PAIR ** -0.5, 0.375, (), jnp.float32)
    return dict(embedded_homologs=embedded_homologs, group_active_tallies=group_active_tallies, asking_projector=asking_projector, lookup_projector=lookup_projector, content_projector=content_projector, contact_inner_matrix=contact_inner_matrix, contact_inner_offset=contact_inner_offset, contact_outer_matrix=contact_outer_matrix)


def reference(embedded_homologs, group_active_tallies, asking_projector, lookup_projector, content_projector, contact_inner_matrix, contact_inner_offset, contact_outer_matrix):
    live = (jnp.arange(BLOCK, dtype=jnp.int32)[None, :] < group_active_tallies[:, None]).reshape(SEQUENCE_TOTAL).astype(jnp.float32)
    count = jnp.sum(group_active_tallies.astype(jnp.float32))
    sequence_groups = embedded_homologs.reshape(SEQUENCE_TOTAL // SEQUENCES_EACH, SEQUENCES_EACH, SITE_TOTAL, EMBED_SIZE)
    marks = live.reshape(SEQUENCE_TOTAL // SEQUENCES_EACH, SEQUENCES_EACH)

    def project(homolog_sequences, weight):
        merged_matrix = homolog_sequences.reshape(SEQUENCES_EACH * SITE_TOTAL, EMBED_SIZE)
        made = jnp.dot(merged_matrix, weight, preferred_element_type=jnp.float32).astype(jnp.bfloat16)
        return made.reshape(SEQUENCES_EACH, SITE_TOTAL, HEADS, HEAD_DIM)

    def add_logits(total, items):
        homolog_sequences, marked = items
        query = project(homolog_sequences, asking_projector).astype(jnp.float32) * marked[:, None, None, None]
        key = project(homolog_sequences, lookup_projector).astype(jnp.float32)
        return (total + jnp.einsum('rihd,rjhd->hij', query, key), 0)
    start = jnp.zeros((HEADS, SITE_TOTAL, SITE_TOTAL), jnp.float32)
    logits, unused = lax.scan(add_logits, start, (sequence_groups, marks))
    maps = jax.nn.softmax(logits / jnp.sqrt(HEAD_DIM * count), axis=-1).astype(jnp.bfloat16)
    maps_wide = maps.astype(jnp.float32)

    def apply_maps(homolog_sequences):
        value = project(homolog_sequences, content_projector).astype(jnp.float32)
        result = jnp.einsum('hij,rjhd->rihd', maps_wide, value)
        return result.astype(jnp.bfloat16).reshape(SEQUENCES_EACH, SITE_TOTAL, EMBED_SIZE)
    attended = lax.map(apply_maps, sequence_groups).reshape(SEQUENCE_TOTAL, SITE_TOTAL, EMBED_SIZE)
    feature = (SITE_TOTAL * maps_wide).transpose(1, 2, 0).reshape(SITE_TOTAL * SITE_TOTAL, HEADS)
    hidden = jax.nn.gelu(jnp.dot(feature, contact_inner_matrix, precision=lax.Precision.HIGHEST) + contact_inner_offset)
    pair = jnp.dot(hidden, contact_outer_matrix, precision=lax.Precision.HIGHEST).astype(jnp.bfloat16).reshape(SITE_TOTAL, SITE_TOTAL, PAIR)
    return (attended, pair)
```

```python
import jax
import jax.numpy as jnp
from jax import lax
from jax.sharding import PartitionSpec as P

HEAD_DIM = 64
BLOCK = 8


def project(merged_matrix, weight, homolog_sequences, sequence_extent):
    made = jnp.dot(merged_matrix, weight, preferred_element_type=jnp.float32).astype(jnp.bfloat16)
    return made.reshape(homolog_sequences, sequence_extent, weight.shape[1] // HEAD_DIM, HEAD_DIM)


def body(
    embedded_homologs,
    group_active_tallies,
    asking_projector,
    lookup_projector,
    content_projector,
    contact_inner_matrix,
    contact_inner_offset,
    contact_outer_matrix,
):
    homolog_sequences, sequence_extent, channel_extent = embedded_homologs.shape
    merged_matrix = embedded_homologs.reshape(homolog_sequences * sequence_extent, channel_extent)
    marked = (
        (jnp.arange(BLOCK, dtype=jnp.int32)[None, :] < group_active_tallies[:, None])
        .reshape(homolog_sequences)
        .astype(jnp.bfloat16)
    )
    query = (
        project(merged_matrix, asking_projector, homolog_sequences, sequence_extent)
        * marked[:, None, None, None]
    )
    key = project(merged_matrix, lookup_projector, homolog_sequences, sequence_extent)
    partial_logits = jnp.einsum("rihd,rjhd->hij", query, key, preferred_element_type=jnp.float32)
    groups = lax.axis_size("depth")
    heads_here = partial_logits.shape[0]
    rows = sequence_extent // groups
    sent = (
        partial_logits.reshape(heads_here, groups, rows, sequence_extent)
        .transpose(1, 0, 2, 3)
        .astype(jnp.bfloat16)
        .reshape(groups, heads_here * rows, sequence_extent)
    )
    tally = jnp.sum(group_active_tallies.astype(jnp.float32)).astype(jnp.bfloat16)
    sent = jnp.concatenate([sent, jnp.full((groups, 8, sequence_extent), tally, jnp.bfloat16)], axis=1)
    got = lax.all_to_all(sent, "depth", split_axis=0, concat_axis=0, tiled=True)
    total = jnp.sum(got.astype(jnp.float32), axis=0)
    count = total[heads_here * rows, 0]
    scale = 1.0 / jnp.sqrt(HEAD_DIM * count)
    own = jax.nn.softmax(total[: heads_here * rows] * scale, axis=-1).astype(jnp.bfloat16)
    own = jnp.broadcast_to(own[None], (groups,) + own.shape)
    maps = lax.all_to_all(own, "depth", split_axis=0, concat_axis=0, tiled=True)
    maps = (
        maps.reshape(groups, heads_here, rows, sequence_extent)
        .transpose(1, 0, 2, 3)
        .reshape(heads_here, sequence_extent, sequence_extent)
    )
    value = project(merged_matrix, content_projector, homolog_sequences, sequence_extent)
    attended = jnp.einsum("hij,rjhd->rihd", maps, value, preferred_element_type=jnp.float32)
    attended = attended.astype(jnp.bfloat16).reshape(
        homolog_sequences, sequence_extent, content_projector.shape[1]
    )
    columns = sequence_extent // lax.axis_size("depth")
    begin = lax.axis_index("depth") * columns
    tile = lax.dynamic_slice_in_dim(maps, begin, columns, 2)
    regrouped = lax.all_to_all(tile, "head", split_axis=1, concat_axis=0, tiled=True)
    heads_all, tile_rows, tile_cols = regrouped.shape
    feature = (
        (sequence_extent * regrouped.astype(jnp.float32))
        .transpose(1, 2, 0)
        .reshape(tile_rows * tile_cols, heads_all)
    )
    hidden = jax.nn.gelu(
        jnp.dot(feature, contact_inner_matrix, precision=lax.Precision.HIGHEST)
        + contact_inner_offset
    )
    pair = jnp.dot(hidden, contact_outer_matrix, precision=lax.Precision.HIGHEST).astype(
        jnp.bfloat16
    )
    return (attended, pair.reshape(tile_rows, tile_cols, contact_outer_matrix.shape[1]))


def solution(mesh):
    return jax.shard_map(
        body,
        mesh=mesh,
        in_specs=(
            P("depth", None, None),
            P("depth"),
            P(None, "head"),
            P(None, "head"),
            P(None, "head"),
            P(),
            P(),
            P(),
        ),
        out_specs=(P("depth", None, "head"), P("head", "depth", None)),
        check_vma=False,
    )
```

```python
import functools

import jax
import jax.numpy as jnp
from jax import lax
from jax.experimental import pallas as pl
from jax.experimental.pallas import tpu as pltpu
from jax.sharding import PartitionSpec as P

HEAD_DIM = 64
BLOCK = 8
LANES = 128
CHUNK = 4

NT = (((1,), (1,)), ((), ()))
TN = (((0,), (0,)), ((), ()))
F32 = jnp.float32
BF16 = jnp.bfloat16


def dot(a, b, dims):
    return lax.dot_general(a, b, dims, preferred_element_type=F32)


def split_words(a):
    high = a.astype(BF16)
    return high, (a - high.astype(F32)).astype(BF16)


def kernel(
    groups,
    teams,
    tallies,
    x_hbm,
    wq_hbm,
    wk_hbm,
    wv_hbm,
    inner,
    offset,
    outer,
    attended,
    pair,
    x,
    w,
    qs,
    ks,
    vs,
    sums,
    sums_in,
    maps_all,
    counts,
    tile_out,
    tile_in,
    x_sem,
    w_sem,
    count_sem,
    sum_sem,
    map_sem,
    tile_send,
    tile_recv,
):
    rows, sites, width = x.shape
    made = w.shape[0] // 3
    heads = made // HEAD_DIM
    own_rows = sites // groups
    me = lax.axis_index("depth")
    team = lax.axis_index("head")
    steps = rows // CHUNK

    def x_copy(c):
        part = pl.ds(c * CHUNK, CHUNK)
        return pltpu.make_async_copy(x_hbm.at[part], x.at[part], x_sem.at[c])

    def w_copy(n):
        return pltpu.make_async_copy(
            (wq_hbm, wk_hbm, wv_hbm)[n], w.at[pl.ds(n * made, made)], w_sem.at[n]
        )

    w_copy(0).start()
    w_copy(1).start()
    for c in range(steps):
        x_copy(c).start()
    w_copy(2).start()

    barrier = pltpu.get_barrier_semaphore()

    def greet(k, carry):
        pl.semaphore_signal(barrier, inc=1, device_id=(lax.rem(me + k, groups), team), device_id_type=pl.DeviceIdType.MESH)
        return carry

    lax.fori_loop(1, groups, greet, 0)
    for k in range(1, teams):
        pl.semaphore_signal(barrier, inc=1, device_id=(me, lax.rem(team + k, teams)), device_id_type=pl.DeviceIdType.MESH)

    w_copy(0).wait()
    w_copy(1).wait()

    def project_qk(c, carry):
        x_copy(c).wait()
        for n in range(CHUNK):
            r = c * CHUNK + n
            live = jnp.where(lax.rem(r, BLOCK) < tallies[r // BLOCK], 1.0, 0.0)
            qk = dot(w[: 2 * made], x[r], NT)
            q = (qk[:made] * live).astype(BF16)
            k = qk[made:].astype(BF16)
            for h in range(heads):
                place = pl.ds(r * HEAD_DIM, HEAD_DIM)
                qs[h, place, :] = q[h * HEAD_DIM : (h + 1) * HEAD_DIM]
                ks[h, place, :] = k[h * HEAD_DIM : (h + 1) * HEAD_DIM]
        return carry

    lax.fori_loop(0, steps, project_qk, 0)

    count = jnp.float32(0)
    for n in range(rows // BLOCK):
        count += tallies[n].astype(F32)
    counts[me] = jnp.full(counts.shape[1:], count, F32)
    pl.semaphore_wait(barrier, groups - 1 + teams - 1)

    def count_copy(k):
        return pltpu.make_async_remote_copy(
            src_ref=counts.at[me],
            dst_ref=counts.at[me],
            send_sem=count_sem.at[0],
            recv_sem=count_sem.at[1],
            device_id=(lax.rem(me + k, groups), team),
            device_id_type=pl.DeviceIdType.MESH,
        )

    lax.fori_loop(1, groups, lambda k, carry: (count_copy(k).start(), carry)[1], 0)

    for h in range(heads):
        logits = dot(qs[h], ks[h], TN)
        halves = [
            logits[:, n * LANES : (n + 1) * LANES].reshape(groups, own_rows, LANES)
            for n in range(sites // LANES)
        ]
        deep = own_rows * len(halves)
        sums[:, h * deep : (h + 1) * deep, :] = jnp.concatenate(halves, axis=1).astype(BF16)

    def sum_copy(k):
        to = lax.rem(me + k, groups)
        return pltpu.make_async_remote_copy(
            src_ref=sums.at[to],
            dst_ref=sums_in.at[k - 1],
            send_sem=sum_sem.at[0],
            recv_sem=sum_sem.at[1],
            device_id=(to, team),
            device_id_type=pl.DeviceIdType.MESH,
        )

    lax.fori_loop(1, groups, lambda k, carry: (sum_copy(k).start(), carry)[1], 0)

    w_copy(2).wait()

    def project_v(c, carry):
        for n in range(CHUNK):
            r = c * CHUNK + n
            v = dot(w[2 * made :], x[r], NT).astype(BF16)
            for h in range(heads):
                vs[h, pl.ds(r * HEAD_DIM, HEAD_DIM), :] = v[h * HEAD_DIM : (h + 1) * HEAD_DIM]
        return carry

    lax.fori_loop(0, steps, project_v, 0)

    def wait_all(buffer, sem):
        most = buffer.at[pl.ds(0, groups - 1)]
        pltpu.make_async_copy(most, most, sem).wait()

    wait_all(counts, count_sem.at[1])
    wait_all(sums_in, sum_sem.at[1])
    total_count = jnp.sum(counts[...], axis=0)[:1, :1]
    scale = lax.rsqrt(HEAD_DIM * total_count)
    total = sums[me].astype(F32) + jnp.sum(sums_in[...].astype(F32), axis=0)
    deep = own_rows * (sites // LANES)
    blocks = []
    for h in range(heads):
        part = total[h * deep : (h + 1) * deep] * scale
        left, right = part[:own_rows], part[own_rows:]
        top = jnp.maximum(jnp.max(left, axis=1, keepdims=True), jnp.max(right, axis=1, keepdims=True))
        left, right = jnp.exp(left - top), jnp.exp(right - top)
        whole = jnp.sum(left, axis=1, keepdims=True) + jnp.sum(right, axis=1, keepdims=True)
        blocks += [left / whole, right / whole]
    maps_all[me] = jnp.concatenate(blocks, axis=0).astype(BF16)

    def map_copy(k):
        return pltpu.make_async_remote_copy(
            src_ref=maps_all.at[me],
            dst_ref=maps_all.at[me],
            send_sem=map_sem.at[0],
            recv_sem=map_sem.at[1],
            device_id=(lax.rem(me + k, groups), team),
            device_id_type=pl.DeviceIdType.MESH,
        )

    lax.fori_loop(1, groups, lambda k, carry: (map_copy(k).start(), carry)[1], 0)

    wait_all(maps_all, map_sem.at[1])
    maps = []
    for h in range(heads):
        part = maps_all[:, h * deep : (h + 1) * deep, :].astype(F32)
        maps.append(
            jnp.concatenate(
                [part[:, :own_rows].reshape(sites, LANES), part[:, own_rows:].reshape(sites, LANES)], axis=1
            ).astype(BF16)
        )

    column = lax.broadcasted_iota(jnp.int32, (sites, LANES), 0) - me * own_rows
    lane = lax.broadcasted_iota(jnp.int32, (sites, LANES), 1)
    tile = jnp.zeros((sites, LANES), F32)
    for h in range(heads):
        place = lane - (team * heads + h) * own_rows
        pick = (place == column) & (place >= 0) & (place < own_rows)
        tile += dot(maps[h], pick.astype(F32).astype(BF16), (((1,), (0,)), ((), ())))
    tile_out[...] = tile.astype(BF16).reshape(tile_out.shape)

    def tile_copy(k):
        to = lax.rem(team + k, teams)
        return pltpu.make_async_remote_copy(
            src_ref=tile_out.at[to],
            dst_ref=tile_in.at[k - 1],
            send_sem=tile_send.at[k - 1],
            recv_sem=tile_recv.at[k - 1],
            device_id=(me, to),
            device_id_type=pl.DeviceIdType.MESH,
        )

    for k in range(1, teams):
        tile_copy(k).start()

    for h in range(heads):
        right = maps[h]

        def apply(c, carry):
            place = pl.ds(pl.multiple_of(c * 8 * HEAD_DIM, 8 * HEAD_DIM), 8 * HEAD_DIM)
            out = dot(vs[h, place, :], right, NT).astype(BF16)
            attended[pl.ds(c * 8, 8), h * HEAD_DIM : (h + 1) * HEAD_DIM, :] = out.reshape(8, HEAD_DIM, sites)
            return carry

        lax.fori_loop(0, rows // 8, apply, 0)

    inner_rows = jnp.concatenate(
        [
            jnp.broadcast_to(inner[...][:, None, :], (inner.shape[0], own_rows, inner.shape[1])).reshape(
                inner.shape[0] * own_rows, inner.shape[1]
            ),
            jnp.zeros((LANES - inner.shape[0] * own_rows, inner.shape[1]), F32),
        ],
        axis=0,
    )
    inner_high, inner_low = split_words(inner_rows)
    outer_high, outer_low = split_words(outer[...])
    for k in range(1, teams):
        tile_copy(k).wait_recv()
    tile_sites = sites // teams
    flat = tile_out[team].astype(F32)
    for k in range(1, teams):
        flat += tile_in[k - 1].astype(F32)
    spread = jnp.broadcast_to((flat * sites)[:, None, :], (tile_sites, own_rows, LANES))
    keep = lax.rem(lax.broadcasted_iota(jnp.int32, (tile_sites, own_rows, LANES), 2), own_rows) == (
        lax.broadcasted_iota(jnp.int32, (tile_sites, own_rows, LANES), 1)
    )
    feature = jnp.where(keep, spread, 0.0).reshape(tile_sites * own_rows, LANES).astype(BF16)
    plain = (((1,), (0,)), ((), ()))
    before = dot(feature, inner_high, plain) + dot(feature, inner_low, plain) + offset[...]
    hidden_high, hidden_low = split_words(jax.nn.gelu(before))
    pair[...] = (
        dot(hidden_high, outer_high, plain)
        + dot(hidden_low, outer_high, plain)
        + dot(hidden_high, outer_low, plain)
    ).astype(BF16)

    for k in range(1, teams):
        tile_copy(k).wait_send()
    wait_all(counts, count_sem.at[0])
    wait_all(sums_in, sum_sem.at[0])
    wait_all(maps_all, map_sem.at[0])


def body(
    embedded_homologs,
    group_active_tallies,
    asking_projector,
    lookup_projector,
    content_projector,
    contact_inner_matrix,
    contact_inner_offset,
    contact_outer_matrix,
):
    rows, sites, width = embedded_homologs.shape
    made = asking_projector.shape[1]
    heads = made // HEAD_DIM
    groups, teams = lax.axis_size("depth"), lax.axis_size("head")
    own_rows = sites // groups
    features = contact_inner_matrix.shape[1]
    outputs = contact_outer_matrix.shape[1]
    deep = heads * own_rows * (sites // LANES)
    tile_rows = sites // teams
    anywhere = pl.BlockSpec(memory_space=pl.ANY)
    local = pl.BlockSpec(memory_space=pltpu.VMEM)
    attended, pair = pl.pallas_call(
        functools.partial(kernel, groups, teams),
        out_shape=(
            jax.ShapeDtypeStruct((rows, made, sites), BF16),
            jax.ShapeDtypeStruct((tile_rows * own_rows, outputs), BF16),
        ),
        in_specs=[pl.BlockSpec(memory_space=pltpu.SMEM)] + [anywhere] * 4 + [local] * 3,
        out_specs=(local, local),
        scratch_shapes=[
            pltpu.VMEM((rows, sites, width), BF16),
            pltpu.VMEM((3 * made, width), BF16),
            pltpu.VMEM((heads, rows * HEAD_DIM, sites), BF16),
            pltpu.VMEM((heads, rows * HEAD_DIM, sites), BF16),
            pltpu.VMEM((heads, rows * HEAD_DIM, sites), BF16),
            pltpu.VMEM((groups, deep, LANES), BF16),
            pltpu.VMEM((groups - 1, deep, LANES), BF16),
            pltpu.VMEM((groups, deep, LANES), BF16),
            pltpu.VMEM((groups, 8, LANES), F32),
            pltpu.VMEM((teams, tile_rows, LANES), BF16),
            pltpu.VMEM((teams - 1, tile_rows, LANES), BF16),
            pltpu.SemaphoreType.DMA((rows // CHUNK,)),
            pltpu.SemaphoreType.DMA((3,)),
            pltpu.SemaphoreType.DMA((2,)),
            pltpu.SemaphoreType.DMA((2,)),
            pltpu.SemaphoreType.DMA((2,)),
            pltpu.SemaphoreType.DMA((teams - 1,)),
            pltpu.SemaphoreType.DMA((teams - 1,)),
        ],
        compiler_params=pltpu.CompilerParams(
            collective_id=0, has_side_effects=True, vmem_limit_bytes=52 * 2**20
        ),
        cost_estimate=pl.CostEstimate(
            flops=2 * rows * sites * made * (3 * width + 2 * sites),
            bytes_accessed=2 * rows * sites * (width + made),
            transcendentals=0,
        ),
    )(
        group_active_tallies,
        embedded_homologs,
        asking_projector.T,
        lookup_projector.T,
        content_projector.T,
        contact_inner_matrix,
        contact_inner_offset.reshape(1, features),
        contact_outer_matrix,
    )
    return (attended.transpose(0, 2, 1), pair.reshape(tile_rows, own_rows, outputs))


def solution(mesh):
    return jax.shard_map(
        body,
        mesh=mesh,
        in_specs=(
            P("depth", None, None),
            P("depth"),
            P(None, "head"),
            P(None, "head"),
            P(None, "head"),
            P(),
            P(),
            P(),
        ),
        out_specs=(P("depth", None, "head"), P("head", "depth", None)),
        check_vma=False,
    )
```

```python
import functools

import jax
import jax.numpy as jnp
from jax import lax
from jax.experimental import pallas as pl
from jax.experimental.pallas import tpu as pltpu
from jax.sharding import PartitionSpec as P

HEAD_DIM = 64
BLOCK = 8
LANES = 128
CHUNK = 4

NT = (((1,), (1,)), ((), ()))
TN = (((0,), (0,)), ((), ()))
F32 = jnp.float32
BF16 = jnp.bfloat16


def dot(a, b, dims):
    return lax.dot_general(a, b, dims, preferred_element_type=F32)


def split_words(a):
    high = a.astype(BF16)
    return high, (a - high.astype(F32)).astype(BF16)


def kernel(
    groups,
    teams,
    tallies_hbm,
    x_hbm,
    wq_hbm,
    wk_hbm,
    wv_hbm,
    inner_hbm,
    offset_hbm,
    outer_hbm,
    attended,
    pair,
    tallies,
    inner,
    offset,
    outer,
    x,
    w,
    qs,
    ks,
    vs,
    sums,
    sums_in,
    maps_all,
    counts,
    tile_out,
    tile_in,
    x_sem,
    w_sem,
    small_sem,
    count_sem,
    sum_sem,
    map_sem,
    tile_send,
    tile_recv,
):
    rows, sites, width = x.shape
    made = w.shape[0] // 3
    heads = made // HEAD_DIM
    own_rows = sites // groups
    me = lax.axis_index("depth")
    team = lax.axis_index("head")
    steps = rows // CHUNK

    def x_copy(c):
        part = pl.ds(c * CHUNK, CHUNK)
        return pltpu.make_async_copy(x_hbm.at[part], x.at[part], x_sem.at[c])

    def w_copy(n):
        return pltpu.make_async_copy(
            (wq_hbm, wk_hbm, wv_hbm)[n], w.at[pl.ds(n * made, made)], w_sem.at[n]
        )

    w_copy(0).start()
    w_copy(1).start()
    for c in range(steps):
        x_copy(c).start()
    w_copy(2).start()
    small_copies = [
        pltpu.make_async_copy(source, target, small_sem.at[n])
        for n, (source, target) in enumerate(
            [(tallies_hbm, tallies), (inner_hbm, inner), (offset_hbm, offset), (outer_hbm, outer)]
        )
    ]
    for copy in small_copies:
        copy.start()

    barrier = pltpu.get_barrier_semaphore()

    def greet(k, carry):
        pl.semaphore_signal(barrier, inc=1, device_id=(lax.rem(me + k, groups), team), device_id_type=pl.DeviceIdType.MESH)
        return carry

    lax.fori_loop(1, groups, greet, 0)
    for k in range(1, teams):
        pl.semaphore_signal(barrier, inc=1, device_id=(me, lax.rem(team + k, teams)), device_id_type=pl.DeviceIdType.MESH)

    small_copies[0].wait()
    w_copy(0).wait()
    w_copy(1).wait()

    def project_qk(c, carry):
        x_copy(c).wait()
        for n in range(CHUNK):
            r = c * CHUNK + n
            live = jnp.where(lax.rem(r, BLOCK) < tallies[r // BLOCK], 1.0, 0.0)
            qk = dot(w[: 2 * made], x[r], NT)
            q = (qk[:made] * live).astype(BF16)
            k = qk[made:].astype(BF16)
            for h in range(heads):
                place = pl.ds(r * HEAD_DIM, HEAD_DIM)
                qs[h, place, :] = q[h * HEAD_DIM : (h + 1) * HEAD_DIM]
                ks[h, place, :] = k[h * HEAD_DIM : (h + 1) * HEAD_DIM]
        return carry

    lax.fori_loop(0, steps, project_qk, 0)

    count = jnp.float32(0)
    for n in range(rows // BLOCK):
        count += tallies[n].astype(F32)
    counts[me] = jnp.full(counts.shape[1:], count, F32)
    pl.semaphore_wait(barrier, groups - 1 + teams - 1)

    def count_copy(k):
        return pltpu.make_async_remote_copy(
            src_ref=counts.at[me],
            dst_ref=counts.at[me],
            send_sem=count_sem.at[0],
            recv_sem=count_sem.at[1],
            device_id=(lax.rem(me + k, groups), team),
            device_id_type=pl.DeviceIdType.MESH,
        )

    lax.fori_loop(1, groups, lambda k, carry: (count_copy(k).start(), carry)[1], 0)

    for h in range(heads):
        logits = dot(qs[h], ks[h], TN)
        halves = [
            logits[:, n * LANES : (n + 1) * LANES].reshape(groups, own_rows, LANES)
            for n in range(sites // LANES)
        ]
        deep = own_rows * len(halves)
        sums[:, h * deep : (h + 1) * deep, :] = jnp.concatenate(halves, axis=1).astype(BF16)

    def sum_copy(k):
        to = lax.rem(me + k, groups)
        return pltpu.make_async_remote_copy(
            src_ref=sums.at[to],
            dst_ref=sums_in.at[k - 1],
            send_sem=sum_sem.at[0],
            recv_sem=sum_sem.at[1],
            device_id=(to, team),
            device_id_type=pl.DeviceIdType.MESH,
        )

    lax.fori_loop(1, groups, lambda k, carry: (sum_copy(k).start(), carry)[1], 0)

    w_copy(2).wait()

    def project_v(c, carry):
        for n in range(CHUNK):
            r = c * CHUNK + n
            v = dot(w[2 * made :], x[r], NT).astype(BF16)
            for h in range(heads):
                vs[h, pl.ds(r * HEAD_DIM, HEAD_DIM), :] = v[h * HEAD_DIM : (h + 1) * HEAD_DIM]
        return carry

    lax.fori_loop(0, steps, project_v, 0)

    def wait_all(buffer, sem):
        most = buffer.at[pl.ds(0, groups - 1)]
        pltpu.make_async_copy(most, most, sem).wait()

    wait_all(counts, count_sem.at[1])
    wait_all(sums_in, sum_sem.at[1])
    total_count = jnp.sum(counts[...], axis=0)[:1, :1]
    scale = lax.rsqrt(HEAD_DIM * total_count)
    total = sums[me].astype(F32) + jnp.sum(sums_in[...].astype(F32), axis=0)
    deep = own_rows * (sites // LANES)
    blocks = []
    for h in range(heads):
        part = total[h * deep : (h + 1) * deep] * scale
        left, right = part[:own_rows], part[own_rows:]
        top = jnp.maximum(jnp.max(left, axis=1, keepdims=True), jnp.max(right, axis=1, keepdims=True))
        left, right = jnp.exp(left - top), jnp.exp(right - top)
        whole = jnp.sum(left, axis=1, keepdims=True) + jnp.sum(right, axis=1, keepdims=True)
        blocks += [left / whole, right / whole]
    maps_all[me] = jnp.concatenate(blocks, axis=0).astype(BF16)

    def map_copy(k):
        return pltpu.make_async_remote_copy(
            src_ref=maps_all.at[me],
            dst_ref=maps_all.at[me],
            send_sem=map_sem.at[0],
            recv_sem=map_sem.at[1],
            device_id=(lax.rem(me + k, groups), team),
            device_id_type=pl.DeviceIdType.MESH,
        )

    lax.fori_loop(1, groups, lambda k, carry: (map_copy(k).start(), carry)[1], 0)

    wait_all(maps_all, map_sem.at[1])
    maps = []
    for h in range(heads):
        part = maps_all[:, h * deep : (h + 1) * deep, :].astype(F32)
        maps.append(
            jnp.concatenate(
                [part[:, :own_rows].reshape(sites, LANES), part[:, own_rows:].reshape(sites, LANES)], axis=1
            ).astype(BF16)
        )

    column = lax.broadcasted_iota(jnp.int32, (sites, LANES), 0) - me * own_rows
    lane = lax.broadcasted_iota(jnp.int32, (sites, LANES), 1)
    tile = jnp.zeros((sites, LANES), F32)
    for h in range(heads):
        place = lane - (team * heads + h) * own_rows
        pick = (place == column) & (place >= 0) & (place < own_rows)
        tile += dot(maps[h], pick.astype(F32).astype(BF16), (((1,), (0,)), ((), ())))
    tile_out[...] = tile.astype(BF16).reshape(tile_out.shape)

    def tile_copy(k):
        to = lax.rem(team + k, teams)
        return pltpu.make_async_remote_copy(
            src_ref=tile_out.at[to],
            dst_ref=tile_in.at[k - 1],
            send_sem=tile_send.at[k - 1],
            recv_sem=tile_recv.at[k - 1],
            device_id=(me, to),
            device_id_type=pl.DeviceIdType.MESH,
        )

    for k in range(1, teams):
        tile_copy(k).start()

    for h in range(heads):
        right = maps[h]

        def apply(c, carry):
            place = pl.ds(pl.multiple_of(c * 8 * HEAD_DIM, 8 * HEAD_DIM), 8 * HEAD_DIM)
            out = dot(vs[h, place, :], right, NT).astype(BF16)
            attended[pl.ds(c * 8, 8), h * HEAD_DIM : (h + 1) * HEAD_DIM, :] = out.reshape(8, HEAD_DIM, sites)
            return carry

        lax.fori_loop(0, rows // 8, apply, 0)

    for copy in small_copies[1:]:
        copy.wait()
    inner_rows = jnp.concatenate(
        [
            jnp.broadcast_to(inner[...][:, None, :], (inner.shape[0], own_rows, inner.shape[1])).reshape(
                inner.shape[0] * own_rows, inner.shape[1]
            ),
            jnp.zeros((LANES - inner.shape[0] * own_rows, inner.shape[1]), F32),
        ],
        axis=0,
    )
    inner_high, inner_low = split_words(inner_rows)
    outer_high, outer_low = split_words(outer[...])
    for k in range(1, teams):
        tile_copy(k).wait_recv()
    tile_sites = sites // teams
    flat = tile_out[team].astype(F32)
    for k in range(1, teams):
        flat += tile_in[k - 1].astype(F32)
    spread = jnp.broadcast_to((flat * sites)[:, None, :], (tile_sites, own_rows, LANES))
    keep = lax.rem(lax.broadcasted_iota(jnp.int32, (tile_sites, own_rows, LANES), 2), own_rows) == (
        lax.broadcasted_iota(jnp.int32, (tile_sites, own_rows, LANES), 1)
    )
    feature = jnp.where(keep, spread, 0.0).reshape(tile_sites * own_rows, LANES).astype(BF16)
    plain = (((1,), (0,)), ((), ()))
    before = dot(feature, inner_high, plain) + dot(feature, inner_low, plain) + offset[...][None, :]
    hidden_high, hidden_low = split_words(jax.nn.gelu(before))
    pair[...] = (
        dot(hidden_high, outer_high, plain)
        + dot(hidden_low, outer_high, plain)
        + dot(hidden_high, outer_low, plain)
    ).astype(BF16)

    for k in range(1, teams):
        tile_copy(k).wait_send()
    wait_all(counts, count_sem.at[0])
    wait_all(sums_in, sum_sem.at[0])
    wait_all(maps_all, map_sem.at[0])


def body(
    embedded_homologs,
    group_active_tallies,
    asking_projector,
    lookup_projector,
    content_projector,
    contact_inner_matrix,
    contact_inner_offset,
    contact_outer_matrix,
):
    rows, sites, width = embedded_homologs.shape
    made = asking_projector.shape[1]
    heads = made // HEAD_DIM
    groups, teams = lax.axis_size("depth"), lax.axis_size("head")
    own_rows = sites // groups
    outputs = contact_outer_matrix.shape[1]
    deep = heads * own_rows * (sites // LANES)
    tile_rows = sites // teams
    local = pl.BlockSpec(memory_space=pltpu.VMEM)
    attended, pair = pl.pallas_call(
        functools.partial(kernel, groups, teams),
        out_shape=(
            jax.ShapeDtypeStruct((rows, made, sites), BF16),
            jax.ShapeDtypeStruct((tile_rows * own_rows, outputs), BF16),
        ),
        in_specs=[pl.BlockSpec(memory_space=pltpu.HBM)] * 8,
        out_specs=(local, local),
        scratch_shapes=[
            pltpu.SMEM(group_active_tallies.shape, jnp.int32),
            pltpu.VMEM(contact_inner_matrix.shape, F32),
            pltpu.VMEM(contact_inner_offset.shape, F32),
            pltpu.VMEM(contact_outer_matrix.shape, F32),
            pltpu.VMEM((rows, sites, width), BF16),
            pltpu.VMEM((3 * made, width), BF16),
            pltpu.VMEM((heads, rows * HEAD_DIM, sites), BF16),
            pltpu.VMEM((heads, rows * HEAD_DIM, sites), BF16),
            pltpu.VMEM((heads, rows * HEAD_DIM, sites), BF16),
            pltpu.VMEM((groups, deep, LANES), BF16),
            pltpu.VMEM((groups - 1, deep, LANES), BF16),
            pltpu.VMEM((groups, deep, LANES), BF16),
            pltpu.VMEM((groups, 8, LANES), F32),
            pltpu.VMEM((teams, tile_rows, LANES), BF16),
            pltpu.VMEM((teams - 1, tile_rows, LANES), BF16),
            pltpu.SemaphoreType.DMA((rows // CHUNK,)),
            pltpu.SemaphoreType.DMA((3,)),
            pltpu.SemaphoreType.DMA((4,)),
            pltpu.SemaphoreType.DMA((2,)),
            pltpu.SemaphoreType.DMA((2,)),
            pltpu.SemaphoreType.DMA((2,)),
            pltpu.SemaphoreType.DMA((teams - 1,)),
            pltpu.SemaphoreType.DMA((teams - 1,)),
        ],
        compiler_params=pltpu.CompilerParams(
            collective_id=0, has_side_effects=True, vmem_limit_bytes=36 * 2**20
        ),
        cost_estimate=pl.CostEstimate(
            flops=2 * rows * sites * made * (3 * width + 2 * sites),
            bytes_accessed=2 * rows * sites * (width + made),
            transcendentals=0,
        ),
    )(
        *(
            pltpu.with_memory_space_constraint(operand, pltpu.HBM)
            for operand in (
                group_active_tallies,
                embedded_homologs,
                asking_projector.T,
                lookup_projector.T,
                content_projector.T,
                contact_inner_matrix,
                contact_inner_offset,
                contact_outer_matrix,
            )
        )
    )
    return (attended.transpose(0, 2, 1), pair.reshape(tile_rows, own_rows, outputs))


def solution(mesh):
    return jax.shard_map(
        body,
        mesh=mesh,
        in_specs=(
            P("depth", None, None),
            P("depth"),
            P(None, "head"),
            P(None, "head"),
            P(None, "head"),
            P(),
            P(),
            P(),
        ),
        out_specs=(P("depth", None, "head"), P("head", "depth", None)),
        check_vma=False,
    )
```

```python
import functools

import jax
import jax.numpy as jnp
import numpy as np
from jax import lax
from jax.experimental import pallas as pl
from jax.experimental.pallas import tpu as pltpu
from jax.sharding import PartitionSpec as P

HEAD_DIM = 64
BLOCK = 8
LANES = 128
PARTS = (4, 4, 8, 8, 8)

NT = (((1,), (1,)), ((), ()))
TN = (((0,), (0,)), ((), ()))
NN = (((1,), (0,)), ((), ()))
BOX = (4, 2, 4)
F32 = jnp.float32
BF16 = jnp.bfloat16


def dot(a, b, dims):
    return lax.dot_general(a, b, dims, preferred_element_type=F32)


def farthest_first(shape):
    offsets = [o for o in np.ndindex(*shape) if any(o)]
    return sorted(offsets, key=lambda o: -sum(min(a, n - a) for a, n in zip(o, shape)))


def split_words(a):
    high = a.astype(BF16)
    return high, (a - high.astype(F32)).astype(BF16)


def spread_kernel(
    groups,
    teams,
    tallies_hbm,
    x_hbm,
    wq_hbm,
    wk_hbm,
    wv_hbm,
    inner_hbm,
    outer_hbm,
    attended,
    flat,
    inner_words,
    outer_words,
    tallies,
    inner,
    outer,
    x,
    w,
    qs,
    ks,
    vs,
    sums,
    sums_in,
    maps_all,
    counts_near,
    counts_far,
    tile_out,
    tile_in,
    x_sem,
    w_sem,
    small_sem,
    near_sem,
    far_sem,
    sum_sem,
    map_sem,
    tile_send,
    tile_recv,
):
    rows, sites, width = x.shape
    made = w.shape[0] // 3
    heads = made // HEAD_DIM
    own_rows = sites // groups
    deep = own_rows * (sites // LANES)
    me = lax.axis_index("depth")
    team = lax.axis_index("head")
    place = (me // (BOX[1] * BOX[2]), lax.rem(me // BOX[2], BOX[1]), lax.rem(me, BOX[2]))

    def peer(offset):
        z, y, x_ = (lax.rem(a + o, n) if o else a for a, o, n in zip(place, offset, BOX))
        return (z * BOX[1] + y) * BOX[2] + x_

    peers = farthest_first(BOX)

    def remote(source, target, send_sem, recv_sem, to):
        return pltpu.make_async_remote_copy(
            src_ref=source,
            dst_ref=target,
            send_sem=send_sem,
            recv_sem=recv_sem,
            device_id=to,
            device_id_type=pl.DeviceIdType.MESH,
        )

    def wait_blocks(buffer, number, sem):
        most = buffer.at[pl.ds(0, number)]
        pltpu.make_async_copy(most, most, sem).wait()

    starts = [sum(PARTS[:n]) for n in range(len(PARTS))]

    def x_copy(n):
        part = pl.ds(starts[n], PARTS[n])
        return pltpu.make_async_copy(x_hbm.at[part], x.at[part], x_sem.at[n])

    def w_copy(n):
        return pltpu.make_async_copy(
            (wq_hbm, wk_hbm, wv_hbm)[n], w.at[pl.ds(n * made, made)], w_sem.at[n]
        )

    small_copies = [
        pltpu.make_async_copy(source, target, small_sem.at[n])
        for n, (source, target) in enumerate([(tallies_hbm, tallies), (inner_hbm, inner), (outer_hbm, outer)])
    ]
    w_copy(0).start()
    w_copy(1).start()
    small_copies[0].start()
    for n in range(len(PARTS)):
        x_copy(n).start()
    w_copy(2).start()
    small_copies[1].start()
    small_copies[2].start()

    barrier = pltpu.get_barrier_semaphore()

    def greet(k, carry):
        pl.semaphore_signal(barrier, inc=1, device_id=(lax.rem(me + k, groups), team), device_id_type=pl.DeviceIdType.MESH)
        return carry

    lax.fori_loop(1, groups, greet, 0)
    for k in range(1, teams):
        pl.semaphore_signal(barrier, inc=1, device_id=(me, lax.rem(team + k, teams)), device_id_type=pl.DeviceIdType.MESH)

    near_peers = [o for o in peers if o[0] == 0]
    far_peers = [o for o in peers if o[1] == 0 and o[2] == 0]

    def count_near_copy(n):
        return remote(
            counts_near.at[len(near_peers)], counts_near.at[n], near_sem.at[0], near_sem.at[1], (peer(near_peers[n]), team)
        )

    def count_far_copy(n):
        return remote(
            counts_far.at[len(far_peers)], counts_far.at[n], far_sem.at[0], far_sem.at[1], (peer(far_peers[n]), team)
        )

    small_copies[0].wait()
    w_copy(0).wait()
    w_copy(1).wait()
    for r in range(rows):
        if r in starts:
            x_copy(starts.index(r)).wait()
        if r == starts[-2]:
            count = jnp.float32(0)
            for n in range(rows // BLOCK):
                count += tallies[n].astype(F32)
            counts_near[len(near_peers)] = jnp.full(counts_near.shape[1:], count, F32)
            pl.semaphore_wait(barrier, groups - 1 + teams - 1)
            for n in range(len(near_peers)):
                count_near_copy(n).start()
        live = jnp.where(r % BLOCK < tallies[r // BLOCK], 1.0, 0.0)
        qk = dot(w[: 2 * made], x[r], NT)
        q = (qk[:made] * live).astype(BF16)
        k = qk[made:].astype(BF16)
        for h in range(heads):
            qs[h, r * HEAD_DIM : (r + 1) * HEAD_DIM, :] = q[h * HEAD_DIM : (h + 1) * HEAD_DIM]
            ks[h, r * HEAD_DIM : (r + 1) * HEAD_DIM, :] = k[h * HEAD_DIM : (h + 1) * HEAD_DIM]

    for h in range(heads):
        logits = dot(qs[h], ks[h], TN)
        halves = [
            logits[:, n * LANES : (n + 1) * LANES].reshape(groups, own_rows, LANES)
            for n in range(sites // LANES)
        ]
        sums[:, h * deep : (h + 1) * deep, :] = jnp.concatenate(halves, axis=1).astype(BF16)

    for n, offset in enumerate(peers):
        to = peer(offset)
        remote(sums.at[to], sums_in.at[n], sum_sem.at[0], sum_sem.at[1], (to, team)).start()

    wait_blocks(counts_near, len(near_peers), near_sem.at[1])
    counts_far[len(far_peers)] = jnp.sum(counts_near[...], axis=0)
    for n in range(len(far_peers)):
        count_far_copy(n).start()

    w_copy(2).wait()
    step = rows // 2

    def project_v(c, carry):
        for n in range(step):
            r = c * step + n
            v = dot(w[2 * made :], x[r], NT).astype(BF16)
            for h in range(heads):
                vs[h, pl.ds(r * HEAD_DIM, HEAD_DIM), :] = v[h * HEAD_DIM : (h + 1) * HEAD_DIM]
        return carry

    lax.fori_loop(0, rows // step, project_v, 0)

    wait_blocks(counts_far, len(far_peers), far_sem.at[1])
    scale = lax.rsqrt(HEAD_DIM * jnp.sum(counts_far[...], axis=0)[:1, :1])
    wait_blocks(sums_in, groups - 1, sum_sem.at[1])
    total = sums[me].astype(F32) + jnp.sum(sums_in[...].astype(F32), axis=0)
    blocks = []
    for h in range(heads):
        part = total[h * deep : (h + 1) * deep] * scale
        left, right = part[:own_rows], part[own_rows:]
        top = jnp.maximum(jnp.max(left, axis=1, keepdims=True), jnp.max(right, axis=1, keepdims=True))
        left, right = jnp.exp(left - top), jnp.exp(right - top)
        whole = jnp.sum(left, axis=1, keepdims=True) + jnp.sum(right, axis=1, keepdims=True)
        blocks += [left / whole, right / whole]
    maps_all[me] = jnp.concatenate(blocks, axis=0).astype(BF16)

    for offset in peers:
        remote(maps_all.at[me], maps_all.at[me], map_sem.at[0], map_sem.at[1], (peer(offset), team)).start()

    small_copies[1].wait()
    small_copies[2].wait()
    inner_rows = jnp.broadcast_to(inner[...][:, None, :], (inner.shape[0], own_rows, inner.shape[1]))
    inner_rows = inner_rows.reshape(inner.shape[0] * own_rows, inner.shape[1])
    inner_rows = jnp.concatenate(
        [inner_rows, jnp.zeros((LANES - inner_rows.shape[0], inner.shape[1]), F32)], axis=0
    )
    inner_words[0], inner_words[1] = split_words(inner_rows)
    outer_words[0], outer_words[1] = split_words(outer[...])

    wait_blocks(maps_all, groups - 1, map_sem.at[1])
    maps = []
    for h in range(heads):
        part = maps_all[:, h * deep : (h + 1) * deep, :].astype(F32)
        maps.append(
            jnp.concatenate(
                [part[:, :own_rows].reshape(sites, LANES), part[:, own_rows:].reshape(sites, LANES)], axis=1
            ).astype(BF16)
        )

    column = lax.broadcasted_iota(jnp.int32, (sites, LANES), 0) - me * own_rows
    lane = lax.broadcasted_iota(jnp.int32, (sites, LANES), 1)
    tile = jnp.zeros((sites, LANES), F32)
    for h in range(heads):
        spot = lane - (team * heads + h) * own_rows
        pick = (spot == column) & (spot >= 0) & (spot < own_rows)
        tile += dot(maps[h], pick.astype(F32).astype(BF16), NN)
    tile_out[...] = tile.astype(BF16).reshape(tile_out.shape)

    def tile_copy(k):
        to = lax.rem(team + k, teams)
        return remote(tile_out.at[to], tile_in.at[k - 1], tile_send.at[k - 1], tile_recv.at[k - 1], (me, to))

    for k in range(1, teams):
        tile_copy(k).start()

    for h in range(heads):
        out = dot(vs[h], maps[h], NT).astype(BF16)
        attended[:, h * HEAD_DIM : (h + 1) * HEAD_DIM, :] = out.reshape(rows, HEAD_DIM, sites)

    wait_blocks(counts_near, len(near_peers), near_sem.at[0])
    wait_blocks(counts_far, len(far_peers), far_sem.at[0])
    wait_blocks(sums_in, groups - 1, sum_sem.at[0])
    wait_blocks(maps_all, groups - 1, map_sem.at[0])
    joined = tile_out[team].astype(F32)
    for k in range(1, teams):
        tile_copy(k).wait_recv()
        joined += tile_in[k - 1].astype(F32)
    flat[...] = joined * sites
    for k in range(1, teams):
        tile_copy(k).wait_send()


def pair_kernel(own_rows, attended, flat, inner_words, outer_words, offset, attended_hbm, pair, out_sem):
    pieces = out_sem.shape[0]
    piece = attended.shape[0] // pieces
    copies = [
        pltpu.make_async_copy(
            attended.at[pl.ds(n * piece, piece)], attended_hbm.at[pl.ds(n * piece, piece)], out_sem.at[n]
        )
        for n in range(pieces)
    ]
    for copy in copies:
        copy.start()
    tile_rows = flat.shape[0]
    shape = (tile_rows, own_rows, LANES)
    keep = lax.rem(lax.broadcasted_iota(jnp.int32, shape, 2), own_rows) == lax.broadcasted_iota(jnp.int32, shape, 1)
    feature = jnp.where(keep, jnp.broadcast_to(flat[...][:, None, :], shape), 0.0)
    feature = feature.reshape(tile_rows * own_rows, LANES).astype(BF16)
    before = dot(feature, inner_words[0], NN) + dot(feature, inner_words[1], NN) + offset[...][None, :]
    high, low = split_words(jax.nn.gelu(before))
    pair[...] = (
        dot(high, outer_words[0], NN) + dot(low, outer_words[0], NN) + dot(high, outer_words[1], NN)
    ).astype(BF16)
    for copy in copies:
        copy.wait()


def body(
    embedded_homologs,
    group_active_tallies,
    asking_projector,
    lookup_projector,
    content_projector,
    contact_inner_matrix,
    contact_inner_offset,
    contact_outer_matrix,
):
    rows, sites, width = embedded_homologs.shape
    made = asking_projector.shape[1]
    heads = made // HEAD_DIM
    groups, teams = lax.axis_size("depth"), lax.axis_size("head")
    own_rows = sites // groups
    outputs = contact_outer_matrix.shape[1]
    deep = heads * own_rows * (sites // LANES)
    tile_rows = sites // teams
    local = pl.BlockSpec(memory_space=pltpu.VMEM)
    stacked = (heads, rows * HEAD_DIM, sites)
    attended, flat, inner_words, outer_words = pl.pallas_call(
        functools.partial(spread_kernel, groups, teams),
        out_shape=(
            jax.ShapeDtypeStruct((rows, made, sites), BF16),
            jax.ShapeDtypeStruct((tile_rows, LANES), F32),
            jax.ShapeDtypeStruct((2, LANES, contact_inner_matrix.shape[1]), BF16),
            jax.ShapeDtypeStruct((2,) + contact_outer_matrix.shape, BF16),
        ),
        in_specs=[pl.BlockSpec(memory_space=pltpu.HBM)] * 7,
        out_specs=(local,) * 4,
        scratch_shapes=[
            pltpu.SMEM(group_active_tallies.shape, jnp.int32),
            pltpu.VMEM(contact_inner_matrix.shape, F32),
            pltpu.VMEM(contact_outer_matrix.shape, F32),
            pltpu.VMEM((rows, sites, width), BF16),
            pltpu.VMEM((3 * made, width), BF16),
            pltpu.VMEM(stacked, BF16),
            pltpu.VMEM(stacked, BF16),
            pltpu.VMEM(stacked, BF16),
            pltpu.VMEM((groups, deep, LANES), BF16),
            pltpu.VMEM((groups - 1, deep, LANES), BF16),
            pltpu.VMEM((groups, deep, LANES), BF16),
            pltpu.VMEM((BOX[1] * BOX[2], 8, LANES), F32),
            pltpu.VMEM((BOX[0], 8, LANES), F32),
            pltpu.VMEM((teams, tile_rows, LANES), BF16),
            pltpu.VMEM((teams - 1, tile_rows, LANES), BF16),
            pltpu.SemaphoreType.DMA((len(PARTS),)),
            pltpu.SemaphoreType.DMA((3,)),
            pltpu.SemaphoreType.DMA((3,)),
            pltpu.SemaphoreType.DMA((2,)),
            pltpu.SemaphoreType.DMA((2,)),
            pltpu.SemaphoreType.DMA((2,)),
            pltpu.SemaphoreType.DMA((2,)),
            pltpu.SemaphoreType.DMA((teams - 1,)),
            pltpu.SemaphoreType.DMA((teams - 1,)),
        ],
        compiler_params=pltpu.CompilerParams(
            collective_id=0, has_side_effects=True, vmem_limit_bytes=36 * 2**20
        ),
        cost_estimate=pl.CostEstimate(
            flops=2 * rows * sites * made * (3 * width + 2 * sites),
            bytes_accessed=2 * rows * sites * (width + made),
            transcendentals=0,
        ),
    )(
        *(
            pltpu.with_memory_space_constraint(operand, pltpu.HBM)
            for operand in (
                group_active_tallies,
                embedded_homologs,
                asking_projector.T,
                lookup_projector.T,
                content_projector.T,
                contact_inner_matrix,
                contact_outer_matrix,
            )
        )
    )
    attended, pair = pl.pallas_call(
        functools.partial(pair_kernel, own_rows),
        out_shape=(
            jax.ShapeDtypeStruct(attended.shape, BF16),
            jax.ShapeDtypeStruct((tile_rows * own_rows, outputs), BF16),
        ),
        in_specs=[local] * 5,
        out_specs=(pl.BlockSpec(memory_space=pltpu.HBM), local),
        scratch_shapes=[pltpu.SemaphoreType.DMA((4,))],
        compiler_params=pltpu.CompilerParams(vmem_limit_bytes=16 * 2**20),
        cost_estimate=pl.CostEstimate(
            flops=2 * tile_rows * own_rows * outputs * outputs * 3,
            bytes_accessed=2 * rows * sites * made,
            transcendentals=tile_rows * own_rows * outputs,
        ),
    )(
        *(pltpu.with_memory_space_constraint(operand, pltpu.VMEM) for operand in (attended, flat, inner_words, outer_words)),
        contact_inner_offset,
    )
    return (attended.transpose(0, 2, 1), pair.reshape(tile_rows, own_rows, outputs))


def solution(mesh):
    return jax.shard_map(
        body,
        mesh=mesh,
        in_specs=(
            P("depth", None, None),
            P("depth"),
            P(None, "head"),
            P(None, "head"),
            P(None, "head"),
            P(),
            P(),
            P(),
        ),
        out_specs=(P("depth", None, "head"), P("head", "depth", None)),
        check_vma=False,
    )
```

```python
import functools

import jax
import jax.numpy as jnp
import numpy as np
from jax import lax
from jax.experimental import pallas as pl
from jax.experimental.pallas import tpu as pltpu
from jax.sharding import PartitionSpec as P

HEAD_DIM = 64
BLOCK = 8
LANES = 128
PARTS = (4, 4, 8, 8, 8)

NT = (((1,), (1,)), ((), ()))
TN = (((0,), (0,)), ((), ()))
NN = (((1,), (0,)), ((), ()))
BOX = (4, 2, 4)
F32 = jnp.float32
BF16 = jnp.bfloat16


def dot(a, b, dims):
    return lax.dot_general(a, b, dims, preferred_element_type=F32)


def farthest_first(shape):
    offsets = [o for o in np.ndindex(*shape) if any(o)]
    return sorted(offsets, key=lambda o: -sum(min(a, n - a) for a, n in zip(o, shape)))


def split_words(a):
    high = a.astype(BF16)
    return high, (a - high.astype(F32)).astype(BF16)


def spread_kernel(
    groups,
    teams,
    tallies_hbm,
    x_hbm,
    wq_hbm,
    wk_hbm,
    wv_hbm,
    inner_hbm,
    outer_hbm,
    vs,
    maps,
    flat,
    inner_words,
    outer_words,
    tallies,
    inner,
    outer,
    x,
    w,
    qs,
    ks,
    sums,
    sums_in,
    maps_all,
    counts_near,
    counts_far,
    tile_out,
    tile_in,
    x_sem,
    w_sem,
    small_sem,
    near_sem,
    far_sem,
    sum_sem,
    map_sem,
    tile_sem,
):
    rows, sites, width = x.shape
    made = w.shape[0] // 3
    heads = made // HEAD_DIM
    own_rows = sites // groups
    deep = own_rows * (sites // LANES)
    me = lax.axis_index("depth")
    team = lax.axis_index("head")
    tile_groups = groups // teams
    tile_team = me // tile_groups
    place = (me // (BOX[1] * BOX[2]), lax.rem(me // BOX[2], BOX[1]), lax.rem(me, BOX[2]))

    def peer(offset):
        z, y, x_ = (lax.rem(a + o, n) if o else a for a, o, n in zip(place, offset, BOX))
        return (z * BOX[1] + y) * BOX[2] + x_

    peers = farthest_first(BOX)

    def remote(source, target, send_sem, recv_sem, to):
        return pltpu.make_async_remote_copy(
            src_ref=source,
            dst_ref=target,
            send_sem=send_sem,
            recv_sem=recv_sem,
            device_id=to,
            device_id_type=pl.DeviceIdType.MESH,
        )

    def wait_blocks(buffer, number, sem):
        most = buffer.at[pl.ds(0, number)]
        pltpu.make_async_copy(most, most, sem).wait()

    starts = [sum(PARTS[:n]) for n in range(len(PARTS))]

    def x_copy(n):
        part = pl.ds(starts[n], PARTS[n])
        return pltpu.make_async_copy(x_hbm.at[part], x.at[part], x_sem.at[n])

    def w_copy(n):
        return pltpu.make_async_copy(
            (wq_hbm, wk_hbm, wv_hbm)[n], w.at[pl.ds(n * made, made)], w_sem.at[n]
        )

    small_copies = [
        pltpu.make_async_copy(source, target, small_sem.at[n])
        for n, (source, target) in enumerate([(tallies_hbm, tallies), (inner_hbm, inner), (outer_hbm, outer)])
    ]
    w_copy(0).start()
    w_copy(1).start()
    small_copies[0].start()
    for n in range(len(PARTS)):
        x_copy(n).start()
    w_copy(2).start()
    small_copies[1].start()
    small_copies[2].start()

    barrier = pltpu.get_barrier_semaphore()

    def greet(to):
        pl.semaphore_signal(barrier, inc=1, device_id=to, device_id_type=pl.DeviceIdType.MESH)

    for offset in peers:
        greet((peer(offset), team))

    def greet_teams():
        for n in range(tile_groups):
            for k in range(1, teams):
                greet((team * tile_groups + n, lax.rem(team + k, teams)))

    near_peers = [o for o in peers if o[0] == 0]
    far_peers = [o for o in peers if o[1] == 0 and o[2] == 0]

    def count_near_copy(n):
        return remote(
            counts_near.at[len(near_peers)], counts_near.at[n], near_sem.at[0], near_sem.at[1], (peer(near_peers[n]), team)
        )

    def count_far_copy(n):
        return remote(
            counts_far.at[len(far_peers)], counts_far.at[n], far_sem.at[0], far_sem.at[1], (peer(far_peers[n]), team)
        )

    small_copies[0].wait()
    w_copy(0).wait()
    w_copy(1).wait()
    for r in range(rows):
        if r in starts:
            x_copy(starts.index(r)).wait()
        if r == starts[1]:
            greet_teams()
        if r == starts[-2]:
            count = jnp.float32(0)
            for n in range(rows // BLOCK):
                count += tallies[n].astype(F32)
            counts_near[len(near_peers)] = jnp.full(counts_near.shape[1:], count, F32)
            pl.semaphore_wait(barrier, jnp.where(tile_team == team, groups - 1, 2 * groups - 1))
            for n in range(len(near_peers)):
                count_near_copy(n).start()
        live = jnp.where(r % BLOCK < tallies[r // BLOCK], 1.0, 0.0)
        qk = dot(w[: 2 * made], x[r], NT)
        q = (qk[:made] * live).astype(BF16)
        k = qk[made:].astype(BF16)
        for h in range(heads):
            qs[h, r * HEAD_DIM : (r + 1) * HEAD_DIM, :] = q[h * HEAD_DIM : (h + 1) * HEAD_DIM]
            ks[h, r * HEAD_DIM : (r + 1) * HEAD_DIM, :] = k[h * HEAD_DIM : (h + 1) * HEAD_DIM]

    for h in range(heads):
        logits = dot(qs[h], ks[h], TN)
        halves = [
            logits[:, n * LANES : (n + 1) * LANES].reshape(groups, own_rows, LANES)
            for n in range(sites // LANES)
        ]
        sums[:, h * deep : (h + 1) * deep, :] = jnp.concatenate(halves, axis=1).astype(BF16)

    for n, offset in enumerate(peers):
        to = peer(offset)
        remote(sums.at[to], sums_in.at[n], sum_sem.at[0], sum_sem.at[1], (to, team)).start()

    wait_blocks(counts_near, len(near_peers), near_sem.at[1])
    counts_far[len(far_peers)] = jnp.sum(counts_near[...], axis=0)
    for n in range(len(far_peers)):
        count_far_copy(n).start()

    w_copy(2).wait()
    step = rows // 2

    def project_v(c, carry):
        for n in range(step):
            r = c * step + n
            v = dot(w[2 * made :], x[r], NT).astype(BF16)
            for h in range(heads):
                vs[h, pl.ds(r * HEAD_DIM, HEAD_DIM), :] = v[h * HEAD_DIM : (h + 1) * HEAD_DIM]
        return carry

    lax.fori_loop(0, rows // step, project_v, 0)

    wait_blocks(counts_far, len(far_peers), far_sem.at[1])
    scale = lax.rsqrt(HEAD_DIM * jnp.sum(counts_far[...], axis=0)[:1, :1])
    wait_blocks(sums_in, groups - 1, sum_sem.at[1])
    total = sums[me].astype(F32) + jnp.sum(sums_in[...].astype(F32), axis=0)
    blocks = []
    for h in range(heads):
        part = total[h * deep : (h + 1) * deep] * scale
        left, right = part[:own_rows], part[own_rows:]
        top = jnp.maximum(jnp.max(left, axis=1, keepdims=True), jnp.max(right, axis=1, keepdims=True))
        left, right = jnp.exp(left - top), jnp.exp(right - top)
        whole = jnp.sum(left, axis=1, keepdims=True) + jnp.sum(right, axis=1, keepdims=True)
        blocks += [left / whole, right / whole]
    maps_all[me] = jnp.concatenate(blocks, axis=0).astype(BF16)

    def spread_map(offset):
        remote(maps_all.at[me], maps_all.at[me], map_sem.at[0], map_sem.at[1], (peer(offset), team)).start()

    def spread_tile(offset):
        to = peer(offset)
        remote(
            tile_out.at[to],
            tile_in.at[team * tile_groups + lax.rem(me, tile_groups)],
            tile_sem.at[0],
            tile_sem.at[1],
            (to, tile_team),
        ).start()

    for offset in peers:
        spread_map(offset)

    shape = (groups, own_rows, sites)
    keep = lax.broadcasted_iota(jnp.int32, shape, 2) // own_rows == lax.broadcasted_iota(jnp.int32, shape, 0)
    column = lax.broadcasted_iota(jnp.int32, (sites, LANES), 0)
    lane = lax.broadcasted_iota(jnp.int32, (sites, LANES), 1)
    tile = jnp.zeros((sites, LANES), F32)
    for h in range(heads):
        both = jnp.concatenate([blocks[2 * h], blocks[2 * h + 1]], axis=1)
        part = jnp.where(keep, jnp.broadcast_to(both[None], shape), 0.0).reshape(sites, sites).astype(BF16)
        pick = lane - (team * heads + h) * own_rows == lax.rem(column, own_rows)
        tile += dot(part, pick.astype(F32).astype(BF16), NN)
    tile_out[...] = tile.reshape(tile_out.shape)
    for offset in peers:
        spread_tile(offset)
    at_home = tile_team == team

    @pl.when(jnp.logical_not(at_home))
    def _():
        spread_tile((0, 0, 0))

    @pl.when(at_home)
    def _():
        pltpu.make_async_copy(
            tile_out.at[me], tile_in.at[team * tile_groups + lax.rem(me, tile_groups)], tile_sem.at[1]
        ).start()

    small_copies[1].wait()
    small_copies[2].wait()
    inner_rows = jnp.broadcast_to(inner[...][:, None, :], (inner.shape[0], own_rows, inner.shape[1]))
    inner_rows = inner_rows.reshape(inner.shape[0] * own_rows, inner.shape[1])
    inner_rows = jnp.concatenate(
        [inner_rows, jnp.zeros((LANES - inner_rows.shape[0], inner.shape[1]), F32)], axis=0
    )
    inner_words[0], inner_words[1] = split_words(inner_rows)
    outer_words[0], outer_words[1] = split_words(outer[...])

    wait_blocks(maps_all, groups - 1, map_sem.at[1])
    for h in range(heads):
        part = maps_all[:, h * deep : (h + 1) * deep, :].astype(F32)
        maps[h] = jnp.concatenate(
            [part[:, :own_rows].reshape(sites, LANES), part[:, own_rows:].reshape(sites, LANES)], axis=1
        ).astype(BF16)

    wait_blocks(tile_in, groups, tile_sem.at[1])
    flat[...] = jnp.sum(tile_in[...].reshape(teams, flat.shape[0], LANES), axis=0) * sites

    wait_blocks(counts_near, len(near_peers), near_sem.at[0])
    wait_blocks(counts_far, len(far_peers), far_sem.at[0])
    wait_blocks(sums_in, groups - 1, sum_sem.at[0])
    wait_blocks(maps_all, groups - 1, map_sem.at[0])

    @pl.when(jnp.logical_not(at_home))
    def _():
        wait_blocks(tile_out, groups, tile_sem.at[0])

    @pl.when(at_home)
    def _():
        wait_blocks(tile_out, groups - 1, tile_sem.at[0])


def apply_kernel(
    own_rows,
    vs,
    maps,
    flat,
    inner_words,
    outer_words,
    offset,
    attended_hbm,
    pair_hbm,
    attended,
    pair,
    out_sem,
):
    heads, _, sites = vs.shape
    rows = attended.shape[0]

    def apply(h):
        part = slice(h * HEAD_DIM, (h + 1) * HEAD_DIM)
        attended[:, part, :] = dot(vs[h], maps[h], NT).astype(BF16).reshape(rows, HEAD_DIM, sites)

    def out_copy(h):
        part = pl.ds(h * HEAD_DIM, HEAD_DIM)
        return pltpu.make_async_copy(attended.at[:, part, :], attended_hbm.at[:, part, :], out_sem.at[h])

    for h in range(heads - 1):
        apply(h)
        out_copy(h).start()

    tile_rows = flat.shape[0]
    shape = (tile_rows, own_rows, LANES)
    keep = lax.rem(lax.broadcasted_iota(jnp.int32, shape, 2), own_rows) == lax.broadcasted_iota(jnp.int32, shape, 1)
    feature = jnp.where(keep, jnp.broadcast_to(flat[...][:, None, :], shape), 0.0)
    feature = feature.reshape(tile_rows * own_rows, LANES).astype(BF16)
    before = dot(feature, inner_words[0], NN) + dot(feature, inner_words[1], NN) + offset[...][None, :]
    high, low = split_words(jax.nn.gelu(before))
    pair[...] = (
        dot(high, outer_words[0], NN) + dot(low, outer_words[0], NN) + dot(high, outer_words[1], NN)
    ).astype(BF16)
    pair_copy = pltpu.make_async_copy(pair, pair_hbm, out_sem.at[heads])
    pair_copy.start()
    apply(heads - 1)
    out_copy(heads - 1).start()
    for h in range(heads):
        out_copy(h).wait()
    pair_copy.wait()


def body(
    embedded_homologs,
    group_active_tallies,
    asking_projector,
    lookup_projector,
    content_projector,
    contact_inner_matrix,
    contact_inner_offset,
    contact_outer_matrix,
):
    rows, sites, width = embedded_homologs.shape
    made = asking_projector.shape[1]
    heads = made // HEAD_DIM
    groups, teams = lax.axis_size("depth"), lax.axis_size("head")
    own_rows = sites // groups
    outputs = contact_outer_matrix.shape[1]
    deep = heads * own_rows * (sites // LANES)
    tile_rows = sites // teams
    local = pl.BlockSpec(memory_space=pltpu.VMEM)
    stacked = (heads, rows * HEAD_DIM, sites)
    held = pl.pallas_call(
        functools.partial(spread_kernel, groups, teams),
        out_shape=(
            jax.ShapeDtypeStruct(stacked, BF16),
            jax.ShapeDtypeStruct((heads, sites, sites), BF16),
            jax.ShapeDtypeStruct((tile_rows, LANES), F32),
            jax.ShapeDtypeStruct((2, LANES, contact_inner_matrix.shape[1]), BF16),
            jax.ShapeDtypeStruct((2,) + contact_outer_matrix.shape, BF16),
        ),
        in_specs=[pl.BlockSpec(memory_space=pltpu.HBM)] * 7,
        out_specs=(local,) * 5,
        scratch_shapes=[
            pltpu.SMEM(group_active_tallies.shape, jnp.int32),
            pltpu.VMEM(contact_inner_matrix.shape, F32),
            pltpu.VMEM(contact_outer_matrix.shape, F32),
            pltpu.VMEM((rows, sites, width), BF16),
            pltpu.VMEM((3 * made, width), BF16),
            pltpu.VMEM(stacked, BF16),
            pltpu.VMEM(stacked, BF16),
            pltpu.VMEM((groups, deep, LANES), BF16),
            pltpu.VMEM((groups - 1, deep, LANES), BF16),
            pltpu.VMEM((groups, deep, LANES), BF16),
            pltpu.VMEM((BOX[1] * BOX[2], 8, LANES), F32),
            pltpu.VMEM((BOX[0], 8, LANES), F32),
            pltpu.VMEM((groups, own_rows, LANES), F32),
            pltpu.VMEM((groups, own_rows, LANES), F32),
            pltpu.SemaphoreType.DMA((len(PARTS),)),
            pltpu.SemaphoreType.DMA((3,)),
            pltpu.SemaphoreType.DMA((3,)),
            pltpu.SemaphoreType.DMA((2,)),
            pltpu.SemaphoreType.DMA((2,)),
            pltpu.SemaphoreType.DMA((2,)),
            pltpu.SemaphoreType.DMA((2,)),
            pltpu.SemaphoreType.DMA((2,)),
        ],
        compiler_params=pltpu.CompilerParams(
            collective_id=0, has_side_effects=True, vmem_limit_bytes=36 * 2**20
        ),
        cost_estimate=pl.CostEstimate(
            flops=2 * rows * sites * made * (3 * width + 2 * sites),
            bytes_accessed=2 * rows * sites * (width + made),
            transcendentals=0,
        ),
    )(
        *(
            pltpu.with_memory_space_constraint(operand, pltpu.HBM)
            for operand in (
                group_active_tallies,
                embedded_homologs,
                asking_projector.T,
                lookup_projector.T,
                content_projector.T,
                contact_inner_matrix,
                contact_outer_matrix,
            )
        )
    )
    attended, pair = pl.pallas_call(
        functools.partial(apply_kernel, own_rows),
        out_shape=(
            jax.ShapeDtypeStruct((rows, made, sites), BF16),
            jax.ShapeDtypeStruct((tile_rows * own_rows, outputs), BF16),
        ),
        in_specs=[local] * 6,
        out_specs=(pl.BlockSpec(memory_space=pltpu.HBM),) * 2,
        scratch_shapes=[
            pltpu.VMEM((rows, made, sites), BF16),
            pltpu.VMEM((tile_rows * own_rows, outputs), BF16),
            pltpu.SemaphoreType.DMA((heads + 1,)),
        ],
        compiler_params=pltpu.CompilerParams(vmem_limit_bytes=16 * 2**20),
        cost_estimate=pl.CostEstimate(
            flops=2 * rows * sites * made * sites,
            bytes_accessed=2 * rows * sites * made,
            transcendentals=tile_rows * own_rows * outputs,
        ),
    )(
        *(pltpu.with_memory_space_constraint(operand, pltpu.VMEM) for operand in held),
        contact_inner_offset,
    )
    return (attended.transpose(0, 2, 1), pair.reshape(tile_rows, own_rows, outputs))


def solution(mesh):
    return jax.shard_map(
        body,
        mesh=mesh,
        in_specs=(
            P("depth", None, None),
            P("depth"),
            P(None, "head"),
            P(None, "head"),
            P(None, "head"),
            P(),
            P(),
            P(),
        ),
        out_specs=(P("depth", None, "head"), P("head", "depth", None)),
        check_vma=False,
    )
```

```python
import functools

import jax
import jax.numpy as jnp
import numpy as np
from jax import lax
from jax.experimental import pallas as pl
from jax.experimental.pallas import tpu as pltpu
from jax.sharding import PartitionSpec as P

HEAD_DIM = 64
BLOCK = 8
LANES = 128
PARTS = (4, 8, 20)

NT = (((1,), (1,)), ((), ()))
TN = (((0,), (0,)), ((), ()))
NN = (((1,), (0,)), ((), ()))
BOX = (4, 2, 4)
F32 = jnp.float32
BF16 = jnp.bfloat16


def dot(a, b, dims):
    return lax.dot_general(a, b, dims, preferred_element_type=F32)


def farthest_first(shape):
    offsets = [o for o in np.ndindex(*shape) if any(o)]
    return sorted(offsets, key=lambda o: -sum(min(a, n - a) for a, n in zip(o, shape)))


def split_words(a):
    high = a.astype(BF16)
    return high, (a - high.astype(F32)).astype(BF16)


def spread_kernel(
    groups,
    teams,
    tallies_hbm,
    x_hbm,
    wq_hbm,
    wk_hbm,
    wv_hbm,
    inner_hbm,
    outer_hbm,
    vs,
    maps,
    flat,
    inner_words,
    outer_word,
    tallies,
    inner,
    outer,
    x,
    w,
    qs,
    ks,
    sums,
    sums_in,
    maps_all,
    counts_near,
    counts_far,
    picks,
    tile_out,
    tile_in,
    x_sem,
    w_sem,
    small_sem,
    near_sem,
    far_sem,
    sum_sem,
    map_sem,
    tile_sem,
):
    rows, sites, width = x.shape
    made = w.shape[0] // 3
    heads = made // HEAD_DIM
    own_rows = sites // groups
    deep = own_rows * (sites // LANES)
    me = lax.axis_index("depth")
    team = lax.axis_index("head")
    tile_groups = groups // teams
    tile_team = me // tile_groups
    place = (me // (BOX[1] * BOX[2]), lax.rem(me // BOX[2], BOX[1]), lax.rem(me, BOX[2]))

    def peer(offset):
        z, y, x_ = (lax.rem(a + o, n) if o else a for a, o, n in zip(place, offset, BOX))
        return (z * BOX[1] + y) * BOX[2] + x_

    peers = farthest_first(BOX)

    def remote(source, target, send_sem, recv_sem, to):
        return pltpu.make_async_remote_copy(
            src_ref=source,
            dst_ref=target,
            send_sem=send_sem,
            recv_sem=recv_sem,
            device_id=to,
            device_id_type=pl.DeviceIdType.MESH,
        )

    def wait_blocks(buffer, number, sem):
        most = buffer.at[pl.ds(0, number)]
        pltpu.make_async_copy(most, most, sem).wait()

    starts = [sum(PARTS[:n]) for n in range(len(PARTS))]

    def x_copy(n):
        part = pl.ds(starts[n], PARTS[n])
        return pltpu.make_async_copy(x_hbm.at[part], x.at[part], x_sem.at[n])

    def w_copy(n):
        return pltpu.make_async_copy(
            (wq_hbm, wk_hbm, wv_hbm)[n], w.at[pl.ds(n * made, made)], w_sem.at[n]
        )

    small_copies = [
        pltpu.make_async_copy(source, target, small_sem.at[n])
        for n, (source, target) in enumerate([(tallies_hbm, tallies), (inner_hbm, inner), (outer_hbm, outer)])
    ]
    w_copy(0).start()
    w_copy(1).start()
    small_copies[0].start()
    x_copy(0).start()
    x_copy(1).start()
    w_copy(2).start()
    small_copies[1].start()
    small_copies[2].start()

    barrier = pltpu.get_barrier_semaphore()

    def greet(to):
        pl.semaphore_signal(barrier, inc=1, device_id=to, device_id_type=pl.DeviceIdType.MESH)

    for offset in peers:
        greet((peer(offset), team))

    def greet_teams():
        for n in range(tile_groups):
            for k in range(1, teams):
                greet((team * tile_groups + n, lax.rem(team + k, teams)))

    near_peers = [o for o in peers if o[0] == 0]
    far_peers = [o for o in peers if o[1] == 0 and o[2] == 0]

    def count_near_copy(n):
        return remote(
            counts_near.at[len(near_peers)], counts_near.at[n], near_sem.at[0], near_sem.at[1], (peer(near_peers[n]), team)
        )

    def count_far_copy(n):
        return remote(
            counts_far.at[len(far_peers)], counts_far.at[n], far_sem.at[0], far_sem.at[1], (peer(far_peers[n]), team)
        )

    small_copies[0].wait()
    w_copy(0).wait()
    w_copy(1).wait()
    for r in range(rows):
        if r in starts:
            n = starts.index(r)
            x_copy(n).wait()
            if n + 2 < len(PARTS):
                x_copy(n + 2).start()
            if n == 1:
                greet_teams()
        live = jnp.where(r % BLOCK < tallies[r // BLOCK], 1.0, 0.0)
        qk = dot(w[: 2 * made], x[r], NT)
        q = (qk[:made] * live).astype(BF16)
        k = qk[made:].astype(BF16)
        for h in range(heads):
            qs[h, r * HEAD_DIM : (r + 1) * HEAD_DIM, :] = q[h * HEAD_DIM : (h + 1) * HEAD_DIM]
            ks[h, r * HEAD_DIM : (r + 1) * HEAD_DIM, :] = k[h * HEAD_DIM : (h + 1) * HEAD_DIM]

    count = jnp.float32(0)
    for n in range(rows // BLOCK):
        count += tallies[n].astype(F32)
    counts_near[len(near_peers)] = jnp.full(counts_near.shape[1:], count, F32)
    pl.semaphore_wait(barrier, jnp.where(tile_team == team, groups - 1, 2 * groups - 1))
    for n in range(len(near_peers)):
        count_near_copy(n).start()

    for h in range(heads):
        logits = dot(qs[h], ks[h], TN)
        halves = [
            logits[:, n * LANES : (n + 1) * LANES].reshape(groups, own_rows, LANES)
            for n in range(sites // LANES)
        ]
        sums[:, h * deep : (h + 1) * deep, :] = jnp.concatenate(halves, axis=1).astype(BF16)

    for n, offset in enumerate(peers):
        to = peer(offset)
        remote(sums.at[to], sums_in.at[n], sum_sem.at[0], sum_sem.at[1], (to, team)).start()

    w_copy(2).wait()
    step = rows // 2

    def project_v(c, carry):
        for n in range(step):
            r = c * step + n
            v = dot(w[2 * made :], x[r], NT).astype(BF16)
            for h in range(heads):
                vs[h, pl.ds(r * HEAD_DIM, HEAD_DIM), :] = v[h * HEAD_DIM : (h + 1) * HEAD_DIM]

        @pl.when(c == 0)
        def _():
            wait_blocks(counts_near, len(near_peers), near_sem.at[1])
            counts_far[len(far_peers)] = jnp.sum(counts_near[...], axis=0)
            for n in range(len(far_peers)):
                count_far_copy(n).start()

        return carry

    lax.fori_loop(0, rows // step, project_v, 0)

    small_copies[1].wait()
    small_copies[2].wait()
    inner_rows = jnp.broadcast_to(inner[...][:, None, :], (inner.shape[0], own_rows, inner.shape[1]))
    inner_rows = inner_rows.reshape(inner.shape[0] * own_rows, inner.shape[1])
    inner_rows = jnp.concatenate(
        [inner_rows, jnp.zeros((LANES - inner_rows.shape[0], inner.shape[1]), F32)], axis=0
    )
    inner_words[:LANES], inner_words[LANES:] = split_words(inner_rows)
    outer_word[...] = outer[...].astype(BF16)
    column = lax.broadcasted_iota(jnp.int32, (sites, LANES), 0)
    lane = lax.broadcasted_iota(jnp.int32, (sites, LANES), 1)
    for h in range(heads):
        pick = lane - (team * heads + h) * own_rows == lax.rem(column, own_rows)
        picks[h] = pick.astype(F32).astype(BF16)

    wait_blocks(counts_far, len(far_peers), far_sem.at[1])
    scale = lax.rsqrt(HEAD_DIM * jnp.sum(counts_far[...], axis=0)[:1, :1])
    wait_blocks(sums_in, groups - 1, sum_sem.at[1])
    total = sums[me].astype(F32) + jnp.sum(sums_in[...].astype(F32), axis=0)
    blocks = []
    for h in range(heads):
        part = total[h * deep : (h + 1) * deep] * scale
        left, right = part[:own_rows], part[own_rows:]
        top = jnp.maximum(jnp.max(left, axis=1, keepdims=True), jnp.max(right, axis=1, keepdims=True))
        left, right = jnp.exp(left - top), jnp.exp(right - top)
        whole = jnp.sum(left, axis=1, keepdims=True) + jnp.sum(right, axis=1, keepdims=True)
        blocks += [left / whole, right / whole]
    maps_all[me] = jnp.concatenate(blocks, axis=0).astype(BF16)

    def spread_map(offset):
        remote(maps_all.at[me], maps_all.at[me], map_sem.at[0], map_sem.at[1], (peer(offset), team)).start()

    def spread_tile(offset):
        to = peer(offset)
        remote(
            tile_out.at[to],
            tile_in.at[team * tile_groups + lax.rem(me, tile_groups)],
            tile_sem.at[0],
            tile_sem.at[1],
            (to, tile_team),
        ).start()

    shape = (groups, own_rows, sites)
    keep = lax.broadcasted_iota(jnp.int32, shape, 2) // own_rows == lax.broadcasted_iota(jnp.int32, shape, 0)
    tile = jnp.zeros((sites, LANES), F32)
    for h in range(heads):
        both = jnp.concatenate([blocks[2 * h], blocks[2 * h + 1]], axis=1)
        part = jnp.where(keep, jnp.broadcast_to(both[None], shape), 0.0).reshape(sites, sites).astype(BF16)
        tile += dot(part, picks[h], NN)
    tile_out[...] = tile.reshape(tile_out.shape)

    for offset in peers:
        spread_tile(offset)
        spread_map(offset)
    at_home = tile_team == team

    @pl.when(jnp.logical_not(at_home))
    def _():
        spread_tile((0, 0, 0))

    @pl.when(at_home)
    def _():
        pltpu.make_async_copy(
            tile_out.at[me], tile_in.at[team * tile_groups + lax.rem(me, tile_groups)], tile_sem.at[1]
        ).start()

    wait_blocks(maps_all, groups - 1, map_sem.at[1])
    for h in range(heads):
        part = maps_all[:, h * deep : (h + 1) * deep, :].astype(F32)
        maps[h] = jnp.concatenate(
            [part[:, :own_rows].reshape(sites, LANES), part[:, own_rows:].reshape(sites, LANES)], axis=1
        ).astype(BF16)

    wait_blocks(tile_in, groups, tile_sem.at[1])
    flat[...] = jnp.sum(tile_in[...].reshape(teams, flat.shape[0], LANES), axis=0) * sites

    wait_blocks(counts_near, len(near_peers), near_sem.at[0])
    wait_blocks(counts_far, len(far_peers), far_sem.at[0])
    wait_blocks(sums_in, groups - 1, sum_sem.at[0])
    wait_blocks(maps_all, groups - 1, map_sem.at[0])

    @pl.when(jnp.logical_not(at_home))
    def _():
        wait_blocks(tile_out, groups, tile_sem.at[0])

    @pl.when(at_home)
    def _():
        wait_blocks(tile_out, groups - 1, tile_sem.at[0])


def apply_kernel(
    own_rows,
    vs,
    maps,
    flat,
    inner_words,
    outer_word,
    offset,
    attended_hbm,
    pair_hbm,
    attended,
    pair,
    out_sem,
):
    heads, _, sites = vs.shape
    rows = attended.shape[0]

    def apply(h):
        part = slice(h * HEAD_DIM, (h + 1) * HEAD_DIM)
        attended[:, part, :] = dot(vs[h], maps[h], NT).astype(BF16).reshape(rows, HEAD_DIM, sites)

    def out_copy(h):
        part = pl.ds(h * HEAD_DIM, HEAD_DIM)
        return pltpu.make_async_copy(attended.at[:, part, :], attended_hbm.at[:, part, :], out_sem.at[h])

    for h in range(heads):
        apply(h)
        out_copy(h).start()

    tile_rows = flat.shape[0]
    shape = (tile_rows, own_rows, LANES)
    keep = lax.rem(lax.broadcasted_iota(jnp.int32, shape, 2), own_rows) == lax.broadcasted_iota(jnp.int32, shape, 1)
    feature = jnp.where(keep, jnp.broadcast_to(flat[...][:, None, :], shape), 0.0)
    feature = feature.reshape(tile_rows * own_rows, LANES).astype(BF16)
    feature = jnp.concatenate([feature, feature], axis=1)
    before = dot(feature, inner_words[...], NN) + offset[...][None, :]
    pair[...] = dot(jax.nn.gelu(before).astype(BF16), outer_word[...], NN).astype(BF16)
    pair_copy = pltpu.make_async_copy(pair, pair_hbm, out_sem.at[heads])
    pair_copy.start()
    for h in range(heads):
        out_copy(h).wait()
    pair_copy.wait()


def body(
    embedded_homologs,
    group_active_tallies,
    asking_projector,
    lookup_projector,
    content_projector,
    contact_inner_matrix,
    contact_inner_offset,
    contact_outer_matrix,
):
    rows, sites, width = embedded_homologs.shape
    made = asking_projector.shape[1]
    heads = made // HEAD_DIM
    groups, teams = lax.axis_size("depth"), lax.axis_size("head")
    own_rows = sites // groups
    outputs = contact_outer_matrix.shape[1]
    deep = heads * own_rows * (sites // LANES)
    tile_rows = sites // teams
    local = pl.BlockSpec(memory_space=pltpu.VMEM)
    stacked = (heads, rows * HEAD_DIM, sites)
    held = pl.pallas_call(
        functools.partial(spread_kernel, groups, teams),
        out_shape=(
            jax.ShapeDtypeStruct(stacked, BF16),
            jax.ShapeDtypeStruct((heads, sites, sites), BF16),
            jax.ShapeDtypeStruct((tile_rows, LANES), F32),
            jax.ShapeDtypeStruct((2 * LANES, contact_inner_matrix.shape[1]), BF16),
            jax.ShapeDtypeStruct(contact_outer_matrix.shape, BF16),
        ),
        in_specs=[pl.BlockSpec(memory_space=pltpu.HBM)] * 7,
        out_specs=(local,) * 5,
        scratch_shapes=[
            pltpu.SMEM(group_active_tallies.shape, jnp.int32),
            pltpu.VMEM(contact_inner_matrix.shape, F32),
            pltpu.VMEM(contact_outer_matrix.shape, F32),
            pltpu.VMEM((rows, sites, width), BF16),
            pltpu.VMEM((3 * made, width), BF16),
            pltpu.VMEM(stacked, BF16),
            pltpu.VMEM(stacked, BF16),
            pltpu.VMEM((groups, deep, LANES), BF16),
            pltpu.VMEM((groups - 1, deep, LANES), BF16),
            pltpu.VMEM((groups, deep, LANES), BF16),
            pltpu.VMEM((BOX[1] * BOX[2], 8, LANES), F32),
            pltpu.VMEM((BOX[0], 8, LANES), F32),
            pltpu.VMEM((heads, sites, LANES), BF16),
            pltpu.VMEM((groups, own_rows, LANES), F32),
            pltpu.VMEM((groups, own_rows, LANES), F32),
            pltpu.SemaphoreType.DMA((len(PARTS),)),
            pltpu.SemaphoreType.DMA((3,)),
            pltpu.SemaphoreType.DMA((3,)),
            pltpu.SemaphoreType.DMA((2,)),
            pltpu.SemaphoreType.DMA((2,)),
            pltpu.SemaphoreType.DMA((2,)),
            pltpu.SemaphoreType.DMA((2,)),
            pltpu.SemaphoreType.DMA((2,)),
        ],
        compiler_params=pltpu.CompilerParams(
            collective_id=0, has_side_effects=True, vmem_limit_bytes=36 * 2**20
        ),
        cost_estimate=pl.CostEstimate(
            flops=2 * rows * sites * made * (3 * width + 2 * sites),
            bytes_accessed=2 * rows * sites * (width + made),
            transcendentals=0,
        ),
    )(
        *(
            pltpu.with_memory_space_constraint(operand, pltpu.HBM)
            for operand in (
                group_active_tallies,
                embedded_homologs,
                asking_projector.T,
                lookup_projector.T,
                content_projector.T,
                contact_inner_matrix,
                contact_outer_matrix,
            )
        )
    )
    attended, pair = pl.pallas_call(
        functools.partial(apply_kernel, own_rows),
        out_shape=(
            jax.ShapeDtypeStruct((rows, made, sites), BF16),
            jax.ShapeDtypeStruct((tile_rows * own_rows, outputs), BF16),
        ),
        in_specs=[local] * 6,
        out_specs=(pl.BlockSpec(memory_space=pltpu.HBM),) * 2,
        scratch_shapes=[
            pltpu.VMEM((rows, made, sites), BF16),
            pltpu.VMEM((tile_rows * own_rows, outputs), BF16),
            pltpu.SemaphoreType.DMA((heads + 1,)),
        ],
        compiler_params=pltpu.CompilerParams(vmem_limit_bytes=16 * 2**20),
        cost_estimate=pl.CostEstimate(
            flops=2 * rows * sites * made * sites,
            bytes_accessed=2 * rows * sites * made,
            transcendentals=tile_rows * own_rows * outputs,
        ),
    )(
        *(pltpu.with_memory_space_constraint(operand, pltpu.VMEM) for operand in held),
        contact_inner_offset,
    )
    return (attended.transpose(0, 2, 1), pair.reshape(tile_rows, own_rows, outputs))


def solution(mesh):
    return jax.shard_map(
        body,
        mesh=mesh,
        in_specs=(
            P("depth", None, None),
            P("depth"),
            P(None, "head"),
            P(None, "head"),
            P(None, "head"),
            P(),
            P(),
            P(),
        ),
        out_specs=(P("depth", None, "head"), P("head", "depth", None)),
        check_vma=False,
    )
```

```python
import functools

import jax
import jax.numpy as jnp
import numpy as np
from jax import lax
from jax.experimental import pallas as pl
from jax.experimental.pallas import tpu as pltpu
from jax.sharding import PartitionSpec as P

HEAD_DIM = 64
BLOCK = 8
LANES = 128
PARTS = (4, 8, 20)

NT = (((1,), (1,)), ((), ()))
TN = (((0,), (0,)), ((), ()))
NN = (((1,), (0,)), ((), ()))
HALVES = 2
SLOT = 32
BOX = (4, 2, 4)
F32 = jnp.float32
BF16 = jnp.bfloat16


def dot(a, b, dims):
    return lax.dot_general(a, b, dims, preferred_element_type=F32)


def farthest_first(shape):
    offsets = [o for o in np.ndindex(*shape) if any(o)]
    return sorted(offsets, key=lambda o: -sum(min(a, n - a) for a, n in zip(o, shape)))


def split_words(a):
    high = a.astype(BF16)
    return high, (a - high.astype(F32)).astype(BF16)


def spread_kernel(
    groups,
    teams,
    tallies_hbm,
    x_hbm,
    wq_hbm,
    wk_hbm,
    wv_hbm,
    inner_hbm,
    outer_hbm,
    vs,
    maps,
    flat,
    inner_words,
    outer_word,
    tallies,
    inner,
    outer,
    x,
    w,
    qs,
    ks,
    sums,
    sums_in,
    maps_all,
    counts_near,
    counts_far,
    picks,
    moves,
    tile_out,
    tile_in,
    x_sem,
    w_sem,
    small_sem,
    near_sem,
    far_sem,
    sum_sem,
    map_sem,
    tile_sem,
):
    rows, sites, width = x.shape
    made = w.shape[0] // 3
    heads = made // HEAD_DIM
    own_rows = sites // groups
    deep = own_rows * (sites // LANES)
    me = lax.axis_index("depth")
    team = lax.axis_index("head")
    tile_groups = groups // teams
    tile_team = me // tile_groups
    place = (me // (BOX[1] * BOX[2]), lax.rem(me // BOX[2], BOX[1]), lax.rem(me, BOX[2]))

    def peer(offset):
        z, y, x_ = (lax.rem(a + o, n) if o else a for a, o, n in zip(place, offset, BOX))
        return (z * BOX[1] + y) * BOX[2] + x_

    peers = farthest_first(BOX)

    def remote(source, target, send_sem, recv_sem, to):
        return pltpu.make_async_remote_copy(
            src_ref=source,
            dst_ref=target,
            send_sem=send_sem,
            recv_sem=recv_sem,
            device_id=to,
            device_id_type=pl.DeviceIdType.MESH,
        )

    def wait_blocks(buffer, number, sem):
        most = buffer.at[pl.ds(0, number)]
        pltpu.make_async_copy(most, most, sem).wait()

    starts = [sum(PARTS[:n]) for n in range(len(PARTS))]

    def x_copy(n):
        part = pl.ds(starts[n], PARTS[n])
        return pltpu.make_async_copy(x_hbm.at[part], x.at[part], x_sem.at[n])

    def w_copy(n):
        return pltpu.make_async_copy(
            (wq_hbm, wk_hbm, wv_hbm)[n], w.at[pl.ds(n * made, made)], w_sem.at[n]
        )

    small_copies = [
        pltpu.make_async_copy(source, target, small_sem.at[n])
        for n, (source, target) in enumerate([(tallies_hbm, tallies), (inner_hbm, inner), (outer_hbm, outer)])
    ]
    w_copy(0).start()
    w_copy(1).start()
    small_copies[0].start()
    x_copy(0).start()
    x_copy(1).start()
    w_copy(2).start()
    small_copies[1].start()
    small_copies[2].start()

    barrier = pltpu.get_barrier_semaphore()

    def greet(to):
        pl.semaphore_signal(barrier, inc=1, device_id=to, device_id_type=pl.DeviceIdType.MESH)

    for offset in peers:
        greet((peer(offset), team))

    def greet_teams():
        for n in range(tile_groups):
            for k in range(1, teams):
                greet((team * tile_groups + n, lax.rem(team + k, teams)))

    near_peers = [o for o in peers if o[0] == 0]
    far_peers = [o for o in peers if o[1] == 0 and o[2] == 0]

    def count_near_copy(n):
        return remote(
            counts_near.at[len(near_peers)], counts_near.at[n], near_sem.at[0], near_sem.at[1], (peer(near_peers[n]), team)
        )

    def count_far_copy(n):
        return remote(
            counts_far.at[len(far_peers)], counts_far.at[n], far_sem.at[0], far_sem.at[1], (peer(far_peers[n]), team)
        )

    small_copies[0].wait()
    w_copy(0).wait()
    w_copy(1).wait()
    for r in range(rows):
        if r in starts:
            n = starts.index(r)
            x_copy(n).wait()
            if n + 2 < len(PARTS):
                x_copy(n + 2).start()
            if n == 1:
                greet_teams()
        live = jnp.where(r % BLOCK < tallies[r // BLOCK], 1.0, 0.0)
        qk = dot(w[: 2 * made], x[r], NT)
        q = (qk[:made] * live).astype(BF16)
        k = qk[made:].astype(BF16)
        for h in range(heads):
            qs[h, r * HEAD_DIM : (r + 1) * HEAD_DIM, :] = q[h * HEAD_DIM : (h + 1) * HEAD_DIM]
            ks[h, r * HEAD_DIM : (r + 1) * HEAD_DIM, :] = k[h * HEAD_DIM : (h + 1) * HEAD_DIM]

    count = jnp.float32(0)
    for n in range(rows // BLOCK):
        count += tallies[n].astype(F32)
    counts_near[len(near_peers)] = jnp.full(counts_near.shape[1:], count, F32)
    pl.semaphore_wait(barrier, jnp.where(tile_team == team, groups - 1, 2 * groups - 1))
    for n in range(len(near_peers)):
        count_near_copy(n).start()

    for h in range(heads):
        logits = dot(qs[h], ks[h], TN)
        halves = [
            logits[:, n * LANES : (n + 1) * LANES].reshape(groups, own_rows, LANES)
            for n in range(sites // LANES)
        ]
        sums[:, h * deep : (h + 1) * deep, :] = jnp.concatenate(halves, axis=1).astype(BF16)

    for n, offset in enumerate(peers):
        to = peer(offset)
        remote(sums.at[to], sums_in.at[n], sum_sem.at[0], sum_sem.at[1], (to, team)).start()

    w_copy(2).wait()
    step = rows // 2

    def project_v(c, carry):
        for n in range(step):
            r = c * step + n
            v = dot(w[2 * made :], x[r], NT).astype(BF16)
            for h in range(heads):
                vs[h, pl.ds(r * HEAD_DIM, HEAD_DIM), :] = v[h * HEAD_DIM : (h + 1) * HEAD_DIM]

        @pl.when(c == 0)
        def _():
            wait_blocks(counts_near, len(near_peers), near_sem.at[1])
            counts_far[len(far_peers)] = jnp.sum(counts_near[...], axis=0)
            for n in range(len(far_peers)):
                count_far_copy(n).start()

        return carry

    lax.fori_loop(0, rows // step, project_v, 0)

    small_copies[1].wait()
    small_copies[2].wait()
    inner_rows = jnp.broadcast_to(inner[...][:, None, :], (inner.shape[0], own_rows, inner.shape[1]))
    inner_rows = inner_rows.reshape(inner.shape[0] * own_rows, inner.shape[1])
    inner_rows = jnp.concatenate(
        [inner_rows, jnp.zeros((LANES - inner_rows.shape[0], inner.shape[1]), F32)], axis=0
    )
    inner_words[:LANES], inner_words[LANES:] = split_words(inner_rows)
    outer_word[...] = outer[...].astype(BF16)
    pairs = own_rows // 2
    shape = (pairs * sites, LANES)
    column = lax.broadcasted_iota(jnp.int32, shape, 0)
    lane = lax.broadcasted_iota(jnp.int32, shape, 1)
    for h in range(heads):
        pick = lane == column // sites * SLOT + h * own_rows + lax.rem(column, own_rows)
        picks[h] = pick.astype(F32).astype(BF16)
    shape = (teams * LANES, LANES)
    column = lax.broadcasted_iota(jnp.int32, shape, 0)
    lane = lax.broadcasted_iota(jnp.int32, shape, 1)
    slot = lax.rem(column, SLOT)
    pick = (lane == column // LANES * (heads * own_rows) + slot) & (slot < heads * own_rows)
    moves[...] = pick.astype(F32).astype(BF16)

    wait_blocks(counts_far, len(far_peers), far_sem.at[1])
    scale = lax.rsqrt(HEAD_DIM * jnp.sum(counts_far[...], axis=0)[:1, :1])
    wait_blocks(sums_in, groups - 1, sum_sem.at[1])
    total = sums[me].astype(F32) + jnp.sum(sums_in[...].astype(F32), axis=0)
    blocks = []
    for h in range(heads):
        part = total[h * deep : (h + 1) * deep] * scale
        left, right = part[:own_rows], part[own_rows:]
        top = jnp.maximum(jnp.max(left, axis=1, keepdims=True), jnp.max(right, axis=1, keepdims=True))
        left, right = jnp.exp(left - top), jnp.exp(right - top)
        whole = jnp.sum(left, axis=1, keepdims=True) + jnp.sum(right, axis=1, keepdims=True)
        blocks += [left / whole, right / whole]
    maps_all[me] = jnp.concatenate(blocks, axis=0).astype(BF16)

    def spread_map(offset):
        remote(maps_all.at[me], maps_all.at[me], map_sem.at[0], map_sem.at[1], (peer(offset), team)).start()

    def spread_tile(offset):
        to = peer(offset)
        remote(
            tile_out.at[to],
            tile_in.at[team * tile_groups + lax.rem(me, tile_groups)],
            tile_sem.at[0],
            tile_sem.at[1],
            (to, tile_team),
        ).start()

    per = own_rows // 2
    shape = (groups // per, own_rows, pairs * sites)
    owner = lax.broadcasted_iota(jnp.int32, shape, 0) * per + lax.broadcasted_iota(jnp.int32, shape, 1) // 2
    keep = lax.rem(lax.broadcasted_iota(jnp.int32, shape, 2), sites) // own_rows == owner
    odd = lax.rem(lax.broadcasted_iota(jnp.int32, (own_rows, sites), 0), 2) == 1
    tile = jnp.zeros((2 * groups, LANES), F32)
    for h in range(heads):
        both = jnp.concatenate([blocks[2 * h], blocks[2 * h + 1]], axis=1)
        wide = jnp.concatenate(
            [
                jnp.where(
                    odd,
                    jnp.broadcast_to(both[2 * n + 1 : 2 * n + 2], odd.shape),
                    jnp.broadcast_to(both[2 * n : 2 * n + 1], odd.shape),
                )
                for n in range(pairs)
            ],
            axis=1,
        )
        part = jnp.where(keep, jnp.broadcast_to(wide[None], shape), 0.0)
        tile += dot(part.reshape(2 * groups, pairs * sites).astype(BF16), picks[h], NN)
    tile_out[...] = tile.reshape(tile_out.shape)

    for offset in peers:
        spread_tile(offset)
    for offset in peers:
        spread_map(offset)
    at_home = tile_team == team

    @pl.when(jnp.logical_not(at_home))
    def _():
        spread_tile((0, 0, 0))

    @pl.when(at_home)
    def _():
        pltpu.make_async_copy(
            tile_out.at[me], tile_in.at[team * tile_groups + lax.rem(me, tile_groups)], tile_sem.at[1]
        ).start()

    wait_blocks(maps_all, groups - 1, map_sem.at[1])
    for h in range(heads):
        part = maps_all[:, h * deep : (h + 1) * deep, :].astype(F32)
        maps[h] = jnp.concatenate(
            [part[:, :own_rows].reshape(sites, LANES), part[:, own_rows:].reshape(sites, LANES)], axis=1
        ).astype(BF16)

    wait_blocks(tile_in, groups, tile_sem.at[1])
    shape = (tile_groups, own_rows, LANES)
    row = lax.broadcasted_iota(jnp.int32, shape, 1)
    keep = lax.broadcasted_iota(jnp.int32, shape, 2) // SLOT == row // 2
    parts = []
    for n in range(teams):
        part = tile_in[n * tile_groups : (n + 1) * tile_groups]
        part = jnp.where(
            lax.rem(row, 2) == 1,
            jnp.broadcast_to(part[:, 1:2], shape),
            jnp.broadcast_to(part[:, 0:1], shape),
        )
        parts.append(jnp.where(keep, part, 0.0).reshape(flat.shape).astype(BF16))
    flat[...] = dot(jnp.concatenate(parts, axis=1), moves[...], NN) * sites

    wait_blocks(counts_near, len(near_peers), near_sem.at[0])
    wait_blocks(counts_far, len(far_peers), far_sem.at[0])
    wait_blocks(sums_in, groups - 1, sum_sem.at[0])
    wait_blocks(maps_all, groups - 1, map_sem.at[0])

    @pl.when(jnp.logical_not(at_home))
    def _():
        wait_blocks(tile_out, groups, tile_sem.at[0])

    @pl.when(at_home)
    def _():
        wait_blocks(tile_out, groups - 1, tile_sem.at[0])


def apply_kernel(
    own_rows,
    vs,
    maps,
    flat,
    inner_words,
    outer_word,
    offset,
    attended_hbm,
    pair_hbm,
    attended,
    pair,
    out_sem,
):
    heads, _, sites = vs.shape
    rows = attended.shape[0]

    def apply(h):
        part = slice(h * HEAD_DIM, (h + 1) * HEAD_DIM)
        attended[:, part, :] = dot(vs[h], maps[h], NT).astype(BF16).reshape(rows, HEAD_DIM, sites)

    def out_copy(h):
        part = pl.ds(h * HEAD_DIM, HEAD_DIM)
        return pltpu.make_async_copy(attended.at[:, part, :], attended_hbm.at[:, part, :], out_sem.at[h])

    for h in range(heads):
        apply(h)
        out_copy(h).start()

    halves = out_sem.shape[0] - heads
    tile_rows = flat.shape[0] // halves
    shape = (tile_rows, own_rows, LANES)
    keep = lax.rem(lax.broadcasted_iota(jnp.int32, shape, 2), own_rows) == lax.broadcasted_iota(jnp.int32, shape, 1)

    def pair_copy(n):
        part = pl.ds(n * tile_rows * own_rows, tile_rows * own_rows)
        return pltpu.make_async_copy(pair.at[part], pair_hbm.at[part], out_sem.at[heads + n])

    for n in range(halves):
        rows_here = flat[n * tile_rows : (n + 1) * tile_rows]
        feature = jnp.where(keep, jnp.broadcast_to(rows_here[:, None, :], shape), 0.0)
        feature = feature.reshape(tile_rows * own_rows, LANES).astype(BF16)
        feature = jnp.concatenate([feature, feature], axis=1)
        before = dot(feature, inner_words[...], NN) + offset[...][None, :]
        out = dot(jax.nn.gelu(before).astype(BF16), outer_word[...], NN).astype(BF16)
        pair[n * tile_rows * own_rows : (n + 1) * tile_rows * own_rows] = out
        pair_copy(n).start()
    for h in range(heads):
        out_copy(h).wait()
    for n in range(halves):
        pair_copy(n).wait()


def body(
    embedded_homologs,
    group_active_tallies,
    asking_projector,
    lookup_projector,
    content_projector,
    contact_inner_matrix,
    contact_inner_offset,
    contact_outer_matrix,
):
    rows, sites, width = embedded_homologs.shape
    made = asking_projector.shape[1]
    heads = made // HEAD_DIM
    groups, teams = lax.axis_size("depth"), lax.axis_size("head")
    own_rows = sites // groups
    outputs = contact_outer_matrix.shape[1]
    deep = heads * own_rows * (sites // LANES)
    tile_rows = sites // teams
    local = pl.BlockSpec(memory_space=pltpu.VMEM)
    stacked = (heads, rows * HEAD_DIM, sites)
    held = pl.pallas_call(
        functools.partial(spread_kernel, groups, teams),
        out_shape=(
            jax.ShapeDtypeStruct(stacked, BF16),
            jax.ShapeDtypeStruct((heads, sites, sites), BF16),
            jax.ShapeDtypeStruct((tile_rows, LANES), F32),
            jax.ShapeDtypeStruct((2 * LANES, contact_inner_matrix.shape[1]), BF16),
            jax.ShapeDtypeStruct(contact_outer_matrix.shape, BF16),
        ),
        in_specs=[pl.BlockSpec(memory_space=pltpu.HBM)] * 7,
        out_specs=(local,) * 5,
        scratch_shapes=[
            pltpu.SMEM(group_active_tallies.shape, jnp.int32),
            pltpu.VMEM(contact_inner_matrix.shape, F32),
            pltpu.VMEM(contact_outer_matrix.shape, F32),
            pltpu.VMEM((rows, sites, width), BF16),
            pltpu.VMEM((3 * made, width), BF16),
            pltpu.VMEM(stacked, BF16),
            pltpu.VMEM(stacked, BF16),
            pltpu.VMEM((groups, deep, LANES), BF16),
            pltpu.VMEM((groups - 1, deep, LANES), BF16),
            pltpu.VMEM((groups, deep, LANES), BF16),
            pltpu.VMEM((BOX[1] * BOX[2], 8, LANES), F32),
            pltpu.VMEM((BOX[0], 8, LANES), F32),
            pltpu.VMEM((heads, own_rows // 2 * sites, LANES), BF16),
            pltpu.VMEM((teams * LANES, LANES), BF16),
            pltpu.VMEM((groups, 2, LANES), F32),
            pltpu.VMEM((groups, 2, LANES), F32),
            pltpu.SemaphoreType.DMA((len(PARTS),)),
            pltpu.SemaphoreType.DMA((3,)),
            pltpu.SemaphoreType.DMA((3,)),
            pltpu.SemaphoreType.DMA((2,)),
            pltpu.SemaphoreType.DMA((2,)),
            pltpu.SemaphoreType.DMA((2,)),
            pltpu.SemaphoreType.DMA((2,)),
            pltpu.SemaphoreType.DMA((2,)),
        ],
        compiler_params=pltpu.CompilerParams(
            collective_id=0, has_side_effects=True, vmem_limit_bytes=36 * 2**20
        ),
        cost_estimate=pl.CostEstimate(
            flops=2 * rows * sites * made * (3 * width + 2 * sites),
            bytes_accessed=2 * rows * sites * (width + made),
            transcendentals=0,
        ),
    )(
        *(
            pltpu.with_memory_space_constraint(operand, pltpu.HBM)
            for operand in (
                group_active_tallies,
                embedded_homologs,
                asking_projector.T,
                lookup_projector.T,
                content_projector.T,
                contact_inner_matrix,
                contact_outer_matrix,
            )
        )
    )
    attended, pair = pl.pallas_call(
        functools.partial(apply_kernel, own_rows),
        out_shape=(
            jax.ShapeDtypeStruct((rows, made, sites), BF16),
            jax.ShapeDtypeStruct((tile_rows * own_rows, outputs), BF16),
        ),
        in_specs=[local] * 6,
        out_specs=(pl.BlockSpec(memory_space=pltpu.HBM),) * 2,
        scratch_shapes=[
            pltpu.VMEM((rows, made, sites), BF16),
            pltpu.VMEM((tile_rows * own_rows, outputs), BF16),
            pltpu.SemaphoreType.DMA((heads + HALVES,)),
        ],
        compiler_params=pltpu.CompilerParams(vmem_limit_bytes=16 * 2**20),
        cost_estimate=pl.CostEstimate(
            flops=2 * rows * sites * made * sites,
            bytes_accessed=2 * rows * sites * made,
            transcendentals=tile_rows * own_rows * outputs,
        ),
    )(
        *(pltpu.with_memory_space_constraint(operand, pltpu.VMEM) for operand in held),
        contact_inner_offset,
    )
    return (attended.transpose(0, 2, 1), pair.reshape(tile_rows, own_rows, outputs))


def solution(mesh):
    return jax.shard_map(
        body,
        mesh=mesh,
        in_specs=(
            P("depth", None, None),
            P("depth"),
            P(None, "head"),
            P(None, "head"),
            P(None, "head"),
            P(),
            P(),
            P(),
        ),
        out_specs=(P("depth", None, "head"), P("head", "depth", None)),
        check_vma=False,
    )
```

```python
import functools

import jax
import jax.numpy as jnp
import numpy as np
from jax import lax
from jax.experimental import pallas as pl
from jax.experimental.pallas import tpu as pltpu
from jax.sharding import PartitionSpec as P

HEAD_DIM = 64
BLOCK = 8
LANES = 128
PARTS = (4, 14, 14)

NT = (((1,), (1,)), ((), ()))
TN = (((0,), (0,)), ((), ()))
NN = (((1,), (0,)), ((), ()))
EARLY = 6
HALVES = 2
SLOT = 32
BOX = (4, 2, 4)
F32 = jnp.float32
BF16 = jnp.bfloat16


def dot(a, b, dims):
    return lax.dot_general(a, b, dims, preferred_element_type=F32)


def farthest_first(shape):
    offsets = [o for o in np.ndindex(*shape) if any(o)]
    return sorted(offsets, key=lambda o: -sum(min(a, n - a) for a, n in zip(o, shape)))


def split_words(a):
    high = a.astype(BF16)
    return high, (a - high.astype(F32)).astype(BF16)


def spread_kernel(
    groups,
    teams,
    tallies_hbm,
    x_hbm,
    wq_hbm,
    wk_hbm,
    wv_hbm,
    inner_hbm,
    outer_hbm,
    vs,
    maps,
    flat,
    inner_words,
    outer_word,
    tallies,
    inner,
    outer,
    x,
    w,
    qs,
    ks,
    sums,
    sums_in,
    maps_all,
    counts_near,
    counts_far,
    picks,
    moves,
    tile_out,
    tile_in,
    x_sem,
    w_sem,
    small_sem,
    near_sem,
    far_sem,
    sum_sem,
    map_sem,
    tile_sem,
):
    rows, sites, width = x.shape
    made = w.shape[0] // 3
    heads = made // HEAD_DIM
    own_rows = sites // groups
    deep = own_rows * (sites // LANES)
    me = lax.axis_index("depth")
    team = lax.axis_index("head")
    tile_groups = groups // teams
    tile_team = me // tile_groups
    place = (me // (BOX[1] * BOX[2]), lax.rem(me // BOX[2], BOX[1]), lax.rem(me, BOX[2]))

    def peer(offset):
        z, y, x_ = (lax.rem(a + o, n) if o else a for a, o, n in zip(place, offset, BOX))
        return (z * BOX[1] + y) * BOX[2] + x_

    peers = farthest_first(BOX)

    def remote(source, target, send_sem, recv_sem, to):
        return pltpu.make_async_remote_copy(
            src_ref=source,
            dst_ref=target,
            send_sem=send_sem,
            recv_sem=recv_sem,
            device_id=to,
            device_id_type=pl.DeviceIdType.MESH,
        )

    def wait_blocks(buffer, number, sem):
        most = buffer.at[pl.ds(0, number)]
        pltpu.make_async_copy(most, most, sem).wait()

    starts = [sum(PARTS[:n]) for n in range(len(PARTS))]

    def x_copy(n):
        part = pl.ds(starts[n], PARTS[n])
        return pltpu.make_async_copy(x_hbm.at[part], x.at[part], x_sem.at[n])

    def w_copy(n):
        return pltpu.make_async_copy(
            (wq_hbm, wk_hbm, wv_hbm)[n], w.at[pl.ds(n * made, made)], w_sem.at[n]
        )

    small_copies = [
        pltpu.make_async_copy(source, target, small_sem.at[n])
        for n, (source, target) in enumerate([(tallies_hbm, tallies), (inner_hbm, inner), (outer_hbm, outer)])
    ]
    w_copy(0).start()
    w_copy(1).start()
    small_copies[0].start()
    x_copy(0).start()
    x_copy(1).start()
    w_copy(2).start()
    small_copies[1].start()
    small_copies[2].start()

    barrier = pltpu.get_barrier_semaphore()

    def greet(to):
        pl.semaphore_signal(barrier, inc=1, device_id=to, device_id_type=pl.DeviceIdType.MESH)

    for offset in peers:
        greet((peer(offset), team))

    def greet_teams():
        for n in range(tile_groups):
            for k in range(1, teams):
                greet((team * tile_groups + n, lax.rem(team + k, teams)))

    near_peers = [o for o in peers if o[0] == 0]
    far_peers = [o for o in peers if o[1] == 0 and o[2] == 0]

    def count_near_copy(n):
        return remote(
            counts_near.at[len(near_peers)], counts_near.at[n], near_sem.at[0], near_sem.at[1], (peer(near_peers[n]), team)
        )

    def count_far_copy(n):
        return remote(
            counts_far.at[len(far_peers)], counts_far.at[n], far_sem.at[0], far_sem.at[1], (peer(far_peers[n]), team)
        )

    small_copies[0].wait()
    w_copy(0).wait()
    w_copy(1).wait()
    for r in range(rows):
        if r in starts:
            n = starts.index(r)
            x_copy(n).wait()
            if n + 2 < len(PARTS):
                x_copy(n + 2).start()
            if n == 1:
                greet_teams()
        live = jnp.where(r % BLOCK < tallies[r // BLOCK], 1.0, 0.0)
        qk = dot(w[: 2 * made], x[r], NT)
        q = (qk[:made] * live).astype(BF16)
        k = qk[made:].astype(BF16)
        for h in range(heads):
            qs[h, r * HEAD_DIM : (r + 1) * HEAD_DIM, :] = q[h * HEAD_DIM : (h + 1) * HEAD_DIM]
            ks[h, r * HEAD_DIM : (r + 1) * HEAD_DIM, :] = k[h * HEAD_DIM : (h + 1) * HEAD_DIM]

    count = jnp.float32(0)
    for n in range(rows // BLOCK):
        count += tallies[n].astype(F32)
    counts_near[len(near_peers)] = jnp.full(counts_near.shape[1:], count, F32)
    pl.semaphore_wait(barrier, jnp.where(tile_team == team, groups - 1, 2 * groups - 1))
    for n in range(len(near_peers)):
        count_near_copy(n).start()

    for h in range(heads):
        logits = dot(qs[h], ks[h], TN)
        halves = [
            logits[:, n * LANES : (n + 1) * LANES].reshape(groups, own_rows, LANES)
            for n in range(sites // LANES)
        ]
        sums[:, h * deep : (h + 1) * deep, :] = jnp.concatenate(halves, axis=1).astype(BF16)

    for n, offset in enumerate(peers):
        to = peer(offset)
        remote(sums.at[to], sums_in.at[n], sum_sem.at[0], sum_sem.at[1], (to, team)).start()

    w_copy(2).wait()
    step = rows // 2

    def project_v(c, carry):
        for n in range(step):
            r = c * step + n
            v = dot(w[2 * made :], x[r], NT).astype(BF16)
            for h in range(heads):
                vs[h, pl.ds(r * HEAD_DIM, HEAD_DIM), :] = v[h * HEAD_DIM : (h + 1) * HEAD_DIM]

        @pl.when(c == 0)
        def _():
            wait_blocks(counts_near, len(near_peers), near_sem.at[1])
            counts_far[len(far_peers)] = jnp.sum(counts_near[...], axis=0)
            for n in range(len(far_peers)):
                count_far_copy(n).start()

        return carry

    lax.fori_loop(0, rows // step, project_v, 0)

    small_copies[1].wait()
    small_copies[2].wait()
    inner_rows = jnp.broadcast_to(inner[...][:, None, :], (inner.shape[0], own_rows, inner.shape[1]))
    inner_rows = inner_rows.reshape(inner.shape[0] * own_rows, inner.shape[1])
    inner_rows = jnp.concatenate(
        [inner_rows, jnp.zeros((LANES - inner_rows.shape[0], inner.shape[1]), F32)], axis=0
    )
    inner_words[:LANES], inner_words[LANES:] = split_words(inner_rows)
    outer_word[...] = outer[...].astype(BF16)
    pairs = own_rows // 2
    shape = (pairs * sites, LANES)
    column = lax.broadcasted_iota(jnp.int32, shape, 0)
    lane = lax.broadcasted_iota(jnp.int32, shape, 1)
    for h in range(heads):
        pick = lane == column // sites * SLOT + h * own_rows + lax.rem(column, own_rows)
        picks[h] = pick.astype(F32).astype(BF16)
    shape = (teams * LANES, LANES)
    column = lax.broadcasted_iota(jnp.int32, shape, 0)
    lane = lax.broadcasted_iota(jnp.int32, shape, 1)
    slot = lax.rem(column, SLOT)
    pick = (lane == column // LANES * (heads * own_rows) + slot) & (slot < heads * own_rows)
    moves[...] = pick.astype(F32).astype(BF16)

    wait_blocks(counts_far, len(far_peers), far_sem.at[1])
    scale = lax.rsqrt(HEAD_DIM * jnp.sum(counts_far[...], axis=0)[:1, :1])
    wait_blocks(sums_in, groups - 1, sum_sem.at[1])
    total = sums[me].astype(F32) + jnp.sum(sums_in[...].astype(F32), axis=0)
    blocks = []
    for h in range(heads):
        part = total[h * deep : (h + 1) * deep] * scale
        left, right = part[:own_rows], part[own_rows:]
        top = jnp.maximum(jnp.max(left, axis=1, keepdims=True), jnp.max(right, axis=1, keepdims=True))
        left, right = jnp.exp(left - top), jnp.exp(right - top)
        whole = jnp.sum(left, axis=1, keepdims=True) + jnp.sum(right, axis=1, keepdims=True)
        blocks += [left / whole, right / whole]
    maps_all[me] = jnp.concatenate(blocks, axis=0).astype(BF16)

    def spread_map(offset):
        remote(maps_all.at[me], maps_all.at[me], map_sem.at[0], map_sem.at[1], (peer(offset), team)).start()

    def spread_tile(offset):
        to = peer(offset)
        remote(
            tile_out.at[to],
            tile_in.at[team * tile_groups + lax.rem(me, tile_groups)],
            tile_sem.at[0],
            tile_sem.at[1],
            (to, tile_team),
        ).start()

    for offset in peers[:EARLY]:
        spread_map(offset)

    per = own_rows // 2
    shape = (groups // per, own_rows, pairs * sites)
    owner = lax.broadcasted_iota(jnp.int32, shape, 0) * per + lax.broadcasted_iota(jnp.int32, shape, 1) // 2
    keep = lax.rem(lax.broadcasted_iota(jnp.int32, shape, 2), sites) // own_rows == owner
    odd = lax.rem(lax.broadcasted_iota(jnp.int32, (own_rows, sites), 0), 2) == 1
    tile = jnp.zeros((2 * groups, LANES), F32)
    for h in range(heads):
        both = jnp.concatenate([blocks[2 * h], blocks[2 * h + 1]], axis=1)
        wide = jnp.concatenate(
            [
                jnp.where(
                    odd,
                    jnp.broadcast_to(both[2 * n + 1 : 2 * n + 2], odd.shape),
                    jnp.broadcast_to(both[2 * n : 2 * n + 1], odd.shape),
                )
                for n in range(pairs)
            ],
            axis=1,
        )
        part = jnp.where(keep, jnp.broadcast_to(wide[None], shape), 0.0)
        tile += dot(part.reshape(2 * groups, pairs * sites).astype(BF16), picks[h], NN)
    tile_out[...] = tile.reshape(tile_out.shape)

    for offset in peers:
        spread_tile(offset)
    for offset in peers[EARLY:]:
        spread_map(offset)
    at_home = tile_team == team

    @pl.when(jnp.logical_not(at_home))
    def _():
        spread_tile((0, 0, 0))

    @pl.when(at_home)
    def _():
        pltpu.make_async_copy(
            tile_out.at[me], tile_in.at[team * tile_groups + lax.rem(me, tile_groups)], tile_sem.at[1]
        ).start()

    wait_blocks(maps_all, groups - 1, map_sem.at[1])
    for h in range(heads):
        part = maps_all[:, h * deep : (h + 1) * deep, :].astype(F32)
        maps[h] = jnp.concatenate(
            [part[:, :own_rows].reshape(sites, LANES), part[:, own_rows:].reshape(sites, LANES)], axis=1
        ).astype(BF16)

    wait_blocks(tile_in, groups, tile_sem.at[1])
    shape = (tile_groups, own_rows, LANES)
    row = lax.broadcasted_iota(jnp.int32, shape, 1)
    keep = lax.broadcasted_iota(jnp.int32, shape, 2) // SLOT == row // 2
    parts = []
    for n in range(teams):
        part = tile_in[n * tile_groups : (n + 1) * tile_groups]
        part = jnp.where(
            lax.rem(row, 2) == 1,
            jnp.broadcast_to(part[:, 1:2], shape),
            jnp.broadcast_to(part[:, 0:1], shape),
        )
        parts.append(jnp.where(keep, part, 0.0).reshape(flat.shape).astype(BF16))
    flat[...] = dot(jnp.concatenate(parts, axis=1), moves[...], NN) * sites

    wait_blocks(counts_near, len(near_peers), near_sem.at[0])
    wait_blocks(counts_far, len(far_peers), far_sem.at[0])
    wait_blocks(sums_in, groups - 1, sum_sem.at[0])
    wait_blocks(maps_all, groups - 1, map_sem.at[0])

    @pl.when(jnp.logical_not(at_home))
    def _():
        wait_blocks(tile_out, groups, tile_sem.at[0])

    @pl.when(at_home)
    def _():
        wait_blocks(tile_out, groups - 1, tile_sem.at[0])


def apply_kernel(
    own_rows,
    vs,
    maps,
    flat,
    inner_words,
    outer_word,
    offset,
    attended_hbm,
    pair_hbm,
    attended,
    pair,
    out_sem,
):
    heads, _, sites = vs.shape
    rows = attended.shape[0]

    def apply(h):
        part = slice(h * HEAD_DIM, (h + 1) * HEAD_DIM)
        attended[:, part, :] = dot(vs[h], maps[h], NT).astype(BF16).reshape(rows, HEAD_DIM, sites)

    def out_copy(h):
        part = pl.ds(h * HEAD_DIM, HEAD_DIM)
        return pltpu.make_async_copy(attended.at[:, part, :], attended_hbm.at[:, part, :], out_sem.at[h])

    for h in range(heads):
        apply(h)
        out_copy(h).start()

    halves = out_sem.shape[0] - heads
    tile_rows = flat.shape[0] // halves
    shape = (tile_rows, own_rows, LANES)
    keep = lax.rem(lax.broadcasted_iota(jnp.int32, shape, 2), own_rows) == lax.broadcasted_iota(jnp.int32, shape, 1)

    def pair_copy(n):
        part = pl.ds(n * tile_rows * own_rows, tile_rows * own_rows)
        return pltpu.make_async_copy(pair.at[part], pair_hbm.at[part], out_sem.at[heads + n])

    for n in range(halves):
        rows_here = flat[n * tile_rows : (n + 1) * tile_rows]
        feature = jnp.where(keep, jnp.broadcast_to(rows_here[:, None, :], shape), 0.0)
        feature = feature.reshape(tile_rows * own_rows, LANES).astype(BF16)
        feature = jnp.concatenate([feature, feature], axis=1)
        before = dot(feature, inner_words[...], NN) + offset[...][None, :]
        out = dot(jax.nn.gelu(before).astype(BF16), outer_word[...], NN).astype(BF16)
        pair[n * tile_rows * own_rows : (n + 1) * tile_rows * own_rows] = out
        pair_copy(n).start()
    for h in range(heads):
        out_copy(h).wait()
    for n in range(halves):
        pair_copy(n).wait()


def body(
    embedded_homologs,
    group_active_tallies,
    asking_projector,
    lookup_projector,
    content_projector,
    contact_inner_matrix,
    contact_inner_offset,
    contact_outer_matrix,
):
    rows, sites, width = embedded_homologs.shape
    made = asking_projector.shape[1]
    heads = made // HEAD_DIM
    groups, teams = lax.axis_size("depth"), lax.axis_size("head")
    own_rows = sites // groups
    outputs = contact_outer_matrix.shape[1]
    deep = heads * own_rows * (sites // LANES)
    tile_rows = sites // teams
    local = pl.BlockSpec(memory_space=pltpu.VMEM)
    stacked = (heads, rows * HEAD_DIM, sites)
    held = pl.pallas_call(
        functools.partial(spread_kernel, groups, teams),
        out_shape=(
            jax.ShapeDtypeStruct(stacked, BF16),
            jax.ShapeDtypeStruct((heads, sites, sites), BF16),
            jax.ShapeDtypeStruct((tile_rows, LANES), F32),
            jax.ShapeDtypeStruct((2 * LANES, contact_inner_matrix.shape[1]), BF16),
            jax.ShapeDtypeStruct(contact_outer_matrix.shape, BF16),
        ),
        in_specs=[pl.BlockSpec(memory_space=pltpu.HBM)] * 7,
        out_specs=(local,) * 5,
        scratch_shapes=[
            pltpu.SMEM(group_active_tallies.shape, jnp.int32),
            pltpu.VMEM(contact_inner_matrix.shape, F32),
            pltpu.VMEM(contact_outer_matrix.shape, F32),
            pltpu.VMEM((rows, sites, width), BF16),
            pltpu.VMEM((3 * made, width), BF16),
            pltpu.VMEM(stacked, BF16),
            pltpu.VMEM(stacked, BF16),
            pltpu.VMEM((groups, deep, LANES), BF16),
            pltpu.VMEM((groups - 1, deep, LANES), BF16),
            pltpu.VMEM((groups, deep, LANES), BF16),
            pltpu.VMEM((BOX[1] * BOX[2], 8, LANES), F32),
            pltpu.VMEM((BOX[0], 8, LANES), F32),
            pltpu.VMEM((heads, own_rows // 2 * sites, LANES), BF16),
            pltpu.VMEM((teams * LANES, LANES), BF16),
            pltpu.VMEM((groups, 2, LANES), F32),
            pltpu.VMEM((groups, 2, LANES), F32),
            pltpu.SemaphoreType.DMA((len(PARTS),)),
            pltpu.SemaphoreType.DMA((3,)),
            pltpu.SemaphoreType.DMA((3,)),
            pltpu.SemaphoreType.DMA((2,)),
            pltpu.SemaphoreType.DMA((2,)),
            pltpu.SemaphoreType.DMA((2,)),
            pltpu.SemaphoreType.DMA((2,)),
            pltpu.SemaphoreType.DMA((2,)),
        ],
        compiler_params=pltpu.CompilerParams(
            collective_id=0, has_side_effects=True, vmem_limit_bytes=36 * 2**20
        ),
        cost_estimate=pl.CostEstimate(
            flops=2 * rows * sites * made * (3 * width + 2 * sites),
            bytes_accessed=2 * rows * sites * (width + made),
            transcendentals=0,
        ),
    )(
        *(
            pltpu.with_memory_space_constraint(operand, pltpu.HBM)
            for operand in (
                group_active_tallies,
                embedded_homologs,
                asking_projector.T,
                lookup_projector.T,
                content_projector.T,
                contact_inner_matrix,
                contact_outer_matrix,
            )
        )
    )
    attended, pair = pl.pallas_call(
        functools.partial(apply_kernel, own_rows),
        out_shape=(
            jax.ShapeDtypeStruct((rows, made, sites), BF16),
            jax.ShapeDtypeStruct((tile_rows * own_rows, outputs), BF16),
        ),
        in_specs=[local] * 6,
        out_specs=(pl.BlockSpec(memory_space=pltpu.HBM),) * 2,
        scratch_shapes=[
            pltpu.VMEM((rows, made, sites), BF16),
            pltpu.VMEM((tile_rows * own_rows, outputs), BF16),
            pltpu.SemaphoreType.DMA((heads + HALVES,)),
        ],
        compiler_params=pltpu.CompilerParams(vmem_limit_bytes=16 * 2**20),
        cost_estimate=pl.CostEstimate(
            flops=2 * rows * sites * made * sites,
            bytes_accessed=2 * rows * sites * made,
            transcendentals=tile_rows * own_rows * outputs,
        ),
    )(
        *(pltpu.with_memory_space_constraint(operand, pltpu.VMEM) for operand in held),
        contact_inner_offset,
    )
    return (attended.transpose(0, 2, 1), pair.reshape(tile_rows, own_rows, outputs))


def solution(mesh):
    return jax.shard_map(
        body,
        mesh=mesh,
        in_specs=(
            P("depth", None, None),
            P("depth"),
            P(None, "head"),
            P(None, "head"),
            P(None, "head"),
            P(),
            P(),
            P(),
        ),
        out_specs=(P("depth", None, "head"), P("head", "depth", None)),
        check_vma=False,
    )
```
